128 devices in a mesh: band: 8 (over y_lo, x), dom: 16 (over z, y_hi, core).
Axes of the slice: x: 4, y: 4 (y_hi: 2, y_lo: 2; y = y_hi * 2 + y_lo), z: 4, core: 2. Of those that a mesh axis runs over, the one named last changes fastest.
Arguments:
- orbitals: bfloat16 [32, 64, 256, 256], P('band', 'dom'), may hold values from -12.5 to 12.5, as said below
- owner_band: int32 [1], replicated, may hold values from 0 to 7
Outputs:
- exchange_field: float32 [32, 64, 256, 256], P('band', 'dom')
- ace_block: float32 [8, 6, 4], P('band')
The draws below stay inside these ranges and needn't reach their ends.
Inputs may be any that keep to these rules, and one draw needn't show every extreme that they name: `orbitals`: real-valued orbital samples, independent from cell to cell.
All inputs are finite; a program needn't handle non-finite values.
Results may differ from the reference program's by a relative error of at most 0.00035.
Values may be sent and summed in bfloat16 or wider, within the bound.
No kernel may reach another device: no remote copies, remote signals or barrier semaphores. Data moves between devices by JAX's collectives and lax.ppermute only.
A program may use at most 256 MiB of HBM per device.

```python
import math
import jax
import jax.numpy as jnp
from jax import lax

NY = 256
NZ = 256
RES = 4
PANEL = 2
SWEEPS = 3
NX = 64
ORBITALS = 32
N_BAND = 8


def draw_orbitals(key, part):
    key = jax.random.fold_in(key, 11)
    shape = (ORBITALS, NX, NY, NZ)
    position = jnp.arange(NX, dtype=jnp.float32) / float(max(NX - 1, 1))
    base = jnp.clip(jax.random.normal(key, shape, jnp.float32), -4.0, 4.0)
    envelope = jnp.exp(jnp.log(2.0) * position)
    field = base * envelope[None, :, None, None]
    return field.astype(jnp.bfloat16)


def setup_inputs(seed: int = 0) -> dict:
    key_list = jax.random.split(jax.random.key(seed), 3)
    return {
        "orbitals": draw_orbitals(jax.random.fold_in(key_list[2], 71), 0),
        "owner_band": jax.random.randint(key_list[1], (1,), 0, N_BAND).astype(jnp.int32),
    }


SCREEN = 0.1


def sweep_weights(count):
    return [1.0 / (1.0 + (6.0 / (6.0 + SCREEN)) * math.cos(math.pi * (2 * sweep + 1) / (2 * count))) for sweep in range(count)]


def operate_on(field):
    summed = jnp.roll(field, 1, 1) + jnp.roll(field, -1, 1)
    summed = summed + jnp.roll(field, 1, 2) + jnp.roll(field, -1, 2)
    summed = summed + jnp.roll(field, 1, 3) + jnp.roll(field, -1, 3)
    return (6.0 + SCREEN) * field - summed


def reference(orbitals, owner_band):
    inverse = 1.0 / (6.0 + SCREEN)
    start_row = (owner_band[0] * RES).astype(jnp.int32)
    panel_float = lax.dynamic_slice_in_dim(orbitals, start_row, PANEL, 0).astype(jnp.float32)
    factors = sweep_weights(SWEEPS)

    def per_orbital(orbital_index):
        orbital = lax.dynamic_index_in_dim(orbitals, orbital_index, 0, keepdims=False).astype(jnp.float32)
        pair_density = panel_float * orbital[None]
        potential = jnp.zeros_like(pair_density)
        for factor in factors:
            potential = potential + factor * ((pair_density - operate_on(potential)) * inverse)
        exchange = -jnp.sum(potential * panel_float, axis=0)
        block_start = ((orbital_index // RES) * RES).astype(jnp.int32)
        resident = lax.dynamic_slice_in_dim(orbitals, block_start, RES, 0).astype(jnp.float32)
        sources = jnp.concatenate([panel_float, resident], axis=0)
        projections = jnp.sum(sources * exchange[None], axis=(1, 2, 3)) / float(NX * NY * NZ)
        return exchange, projections

    exchange_field, projections = lax.map(per_orbital, jnp.arange(ORBITALS, dtype=jnp.int32))
    ace_block = jnp.transpose(projections.reshape(N_BAND, RES, PANEL + RES), (0, 2, 1))
    return exchange_field, ace_block
```

```python
import math

import jax
import jax.numpy as jnp
import numpy as np
from jax import lax
from jax.experimental import pallas as pl
from jax.experimental.pallas import tpu as pltpu
from jax.sharding import PartitionSpec as P

PANEL, SWEEPS, SCREEN = 2, 3, 0.1
PAD = 8
STRIP = 32

def poly():
    d = 6.0 + SCREEN
    w = [1.0 / (1.0 + 6.0 / d * math.cos(math.pi * (2 * k + 1) / (2 * SWEEPS))) for k in range(SWEEPS)]
    p = [w[0] / d]
    for k in range(1, SWEEPS):
        n = [0.0] * (len(p) + 1)
        for i, c in enumerate(p):
            n[i] += c * (1.0 - w[k])
            n[i + 1] += c * w[k] / d
        n[0] += w[k] / d
        p = n
    return p

def mixing(nz, beta):
    near = np.zeros((nz, nz), np.float32)
    far = np.zeros((nz, nz), np.float32)
    for z in range(nz):
        for s, m in ((1, near), (2, far)):
            m[(z - s) % nz, z] += 1.0
            m[(z + s) % nz, z] += 1.0
    return jnp.asarray(np.concatenate([near, near, beta * far], 0)).astype(jnp.bfloat16)

def kernel(o, olo, ohi, p, plo, phi, mix, e, ace, rho, sig, left, base):
    g0, g1, g2 = poly()
    beta = g2 / g1
    kappa = g0 / g1 + 6.0 * beta
    nj, nx, ny, nz = o.shape
    na = p.shape[0]
    steps = ny // STRIP
    f32, bf = jnp.float32, jnp.bfloat16

    def per_orbital(j, _):
        for src_p, src_o, first, count in ((plo, olo, 0, 2), (p, o, 2, nx), (phi, ohi, 2 + nx, 2)):
            def per_plane(k, _):
                for i in range(steps):
                    rows = slice(i * STRIP, (i + 1) * STRIP)
                    ov = src_o[j, k, rows, :].astype(f32)
                    for a in range(na):
                        rho[a, first + k, PAD + i * STRIP:PAD + (i + 1) * STRIP, :] = src_p[a, k, rows, :].astype(f32) * ov
                for a in range(na):
                    rho[a, first + k, PAD - 2:PAD, :] = rho[a, first + k, PAD + ny - 2:PAD + ny, :]
                    rho[a, first + k, PAD + ny:PAD + ny + 2, :] = rho[a, first + k, PAD:PAD + 2, :]
                return 0
            lax.fori_loop(0, count, per_plane, 0)

        def per_out(x, acc):
            for a in range(na):
                for r in range(0, ny + 2 * PAD, 16):
                    sig[a, r:r + 16, :] = rho[a, x + 1, r:r + 16, :] + rho[a, x + 3, r:r + 16, :]
            for a in range(na):
                for i in range(steps):
                    r = PAD + i * STRIP
                    at = lambda ref, idx, s: ref[(*idx, slice(r + s, r + s + STRIP), slice(None))]
                    c = at(rho, (a, x + 2), 0)
                    q = at(sig, (a,), 0) + (at(rho, (a, x + 2), -1) + at(rho, (a, x + 2), 1))
                    far = (at(rho, (a, x), 0) + at(rho, (a, x + 4), 0)) + (at(rho, (a, x + 2), -2) + at(rho, (a, x + 2), 2))
                    side = at(sig, (a,), -1) + at(sig, (a,), 1)
                    v = c + (2.0 * beta) * q
                    hi = v.astype(bf)
                    rows = slice(i * STRIP, (i + 1) * STRIP)
                    left[a, rows, :nz] = hi
                    left[a, rows, nz:2 * nz] = (v - hi.astype(f32)).astype(bf)
                    left[a, rows, 2 * nz:] = c.astype(bf)
                    base[a, rows, :] = (kappa * c + q) + beta * (far + (side + side))
            mixed = [jnp.dot(left[a], mix[...], preferred_element_type=f32) for a in range(na)]
            acc = list(acc)
            for i in range(steps):
                rows = slice(i * STRIP, (i + 1) * STRIP)
                total = None
                pan = []
                for a in range(na):
                    pa = p[a, x, rows, :].astype(f32)
                    pan.append(pa)
                    w = pa * (base[a, rows, :] + mixed[a][rows])
                    total = w if total is None else total + w
                total = total * (-g1)
                e[j, x, rows, :] = total
                for s_i in range(na + nj):
                    src = pan[s_i] if s_i < na else o[s_i - na, x, rows, :].astype(f32)
                    m = src * total
                    m = m[:, :128] + m[:, 128:]
                    acc[s_i] = acc[s_i] + jnp.sum(m.reshape(STRIP // 8, 8, 128), axis=0)
            return tuple(acc)

        acc = lax.fori_loop(0, nx, per_out, tuple(jnp.zeros((8, 128), f32) for _ in range(na + nj)))
        for s_i in range(na + nj):
            ace[j, s_i:s_i + 1, :] = jnp.broadcast_to(jnp.sum(jnp.sum(acc[s_i], axis=0, keepdims=True), axis=1, keepdims=True), (1, 128))
        return 0

    lax.fori_loop(0, nj, per_orbital, 0)

def fields(o, olo, ohi, p, plo, phi):
    nj, nx, ny, nz = o.shape
    na = p.shape[0]
    g = poly()
    vm = pl.BlockSpec(memory_space=pltpu.VMEM)
    return pl.pallas_call(
        kernel,
        out_shape=(jax.ShapeDtypeStruct((nj, nx, ny, nz), jnp.float32), jax.ShapeDtypeStruct((nj, 8, 128), jnp.float32)),
        in_specs=[vm] * 7,
        out_specs=(vm, vm),
        scratch_shapes=[pltpu.VMEM((na, nx + 4, ny + 2 * PAD, nz), jnp.float32), pltpu.VMEM((na, ny + 2 * PAD, nz), jnp.float32),
                        pltpu.VMEM((na, ny, 3 * nz), jnp.bfloat16), pltpu.VMEM((na, ny, nz), jnp.float32)],
        compiler_params=pltpu.CompilerParams(vmem_limit_bytes=40 * 2**20),
    )(o, olo, ohi, p, plo, phi, mixing(nz, g[2] / g[1]))


def ring(count, shift):
    return [(i, (i + shift) % count) for i in range(count)]


def rows(shift, row):
    count = lax.axis_size("band")
    return [(i, i // row * row + (i + shift) % row) for i in range(count)]


def one_plane(array, index):
    return lax.dynamic_slice_in_dim(array, index, 1, 1)


def spread_panel(panel, owner):
    row = panel.shape[1]
    count = lax.axis_size("band")
    me = lax.axis_index("band")
    x, own_x = me % row, owner % row
    got = [one_plane(panel, x)]
    for k in range(1, row):
        got.append(lax.ppermute(one_plane(panel, (x + k) % row), "band", rows(k, row)))
    mine = lax.select_n((x - own_x) % row, *got)
    other = lax.ppermute(mine, "band", ring(count, row))
    mine = jnp.where(me // row == owner // row, mine, other)
    parts = [mine] + [lax.ppermute(mine, "band", rows(k, row)) for k in range(1, row)]
    turned = jnp.concatenate(parts[::-1] + parts[::-1], axis=1)
    return lax.dynamic_slice_in_dim(turned, row - 1 - x, row, 1)


def halos(array, width):
    count = lax.axis_size("dom")
    size = array.shape[1]
    low = lax.ppermute(array[:, size - width:], "dom", ring(count, 1))
    high = lax.ppermute(array[:, :width], "dom", ring(count, -1))
    return low, high


def total(part):
    count = lax.axis_size("dom")
    for group in ((1,), (2,), (4, 8, 12)):
        moved = [lax.ppermute(part, "dom", [(i, i ^ k) for i in range(count)]) for k in group]
        for m in moved:
            part = part + m
    return part


def local(orbitals, owner_band):
    low, high = halos(orbitals, 2)
    panel = spread_panel(orbitals[:PANEL], owner_band[0])
    panel_low, panel_high = halos(panel, 2)
    exchange, sums = fields(orbitals, low, high, panel, panel_low, panel_high)
    cells = float(orbitals.shape[1] * lax.axis_size("dom") * orbitals.shape[2] * orbitals.shape[3])
    sums = total(sums)
    ace_block = jnp.transpose(sums[:, :PANEL + orbitals.shape[0], 0]) / cells
    return exchange, ace_block[None]


def solution(mesh):
    placed = (P("band", "dom", None, None), P())
    return jax.shard_map(
        local,
        mesh=mesh,
        in_specs=placed,
        out_specs=(P("band", "dom", None, None), P("band", None, None)),
        check_vma=False,
    )
```

```python
import math

import jax
import jax.numpy as jnp
import numpy as np
from jax import lax
from jax.experimental import pallas as pl
from jax.experimental.pallas import tpu as pltpu
from jax.sharding import PartitionSpec as P

PANEL, SWEEPS, SCREEN = 2, 3, 0.1
PAD = 8
STRIP = 32


def polynomial():
    d = 6.0 + SCREEN
    w = [1.0 / (1.0 + 6.0 / d * math.cos(math.pi * (2 * k + 1) / (2 * SWEEPS))) for k in range(SWEEPS)]
    p = [w[0] / d]
    for k in range(1, SWEEPS):
        n = [0.0] * (len(p) + 1)
        for i, c in enumerate(p):
            n[i] += c * (1.0 - w[k])
            n[i + 1] += c * w[k] / d
        n[0] += w[k] / d
        p = n
    return p


def mixing(nz, beta):
    near = np.zeros((nz, nz), np.float32)
    far = np.zeros((nz, nz), np.float32)
    for z in range(nz):
        for s, m in ((1, near), (2, far)):
            m[(z - s) % nz, z] += 1.0
            m[(z + s) % nz, z] += 1.0
    return jnp.asarray(np.concatenate([near, near, beta * far], 0)).astype(jnp.bfloat16)


def at(ref, idx, start, size):
    return ref[(*idx, slice(start, start + size), slice(None))]


def wrap(ref, idx, ny, width):
    ref[(*idx, slice(PAD - width, PAD), slice(None))] = at(ref, idx, PAD + ny - width, width)
    ref[(*idx, slice(PAD + ny, PAD + ny + width), slice(None))] = at(ref, idx, PAD, width)


def split(left, a, rows, nz, v):
    hi = v.astype(jnp.bfloat16)
    left[a, rows, :nz] = hi
    left[a, rows, nz:2 * nz] = (v - hi.astype(jnp.float32)).astype(jnp.bfloat16)


def inner_kernel(o, p, mix, e, rho, *scratch):
    g0, g1, g2 = polynomial()
    beta = g2 / g1
    kappa = g0 / g1 + 6.0 * beta
    na, nx, ny, nz = p.shape
    steps = ny // STRIP
    f32, bf = jnp.float32, jnp.bfloat16
    sigs, lefts, bases = scratch[0:2], scratch[2:4], scratch[4:6]

    for x in range(nx):
        for i in range(steps):
            ov = at(o, (0, x), i * STRIP, STRIP).astype(f32)
            for a in range(na):
                rho[a, x, PAD + i * STRIP:PAD + (i + 1) * STRIP, :] = at(p, (a, x), i * STRIP, STRIP).astype(f32) * ov
        for a in range(na):
            wrap(rho, (a, x), ny, 2)

    def prepare(x):
        sig, left, base = sigs[x % 2], lefts[x % 2], bases[x % 2]
        near = [n for n in (x - 1, x + 1) if 0 <= n < nx]
        apart = [n for n in (x - 2, x + 2) if 0 <= n < nx]
        if len(near) > 1:
            for a in range(na):
                for r in range(0, ny + 2 * PAD, 16):
                    sig[a, r:r + 16, :] = at(rho, (a, near[0]), r, 16) + at(rho, (a, near[1]), r, 16)
        for a in range(na):
            s_ref, s_idx = (sig, (a,)) if len(near) > 1 else (rho, (a, near[0]))
            for i in range(steps):
                r = PAD + i * STRIP
                rows = slice(i * STRIP, (i + 1) * STRIP)
                c = at(rho, (a, x), r, STRIP)
                q = at(s_ref, s_idx, r, STRIP) + (at(rho, (a, x), r - 1, STRIP) + at(rho, (a, x), r + 1, STRIP))
                far = at(rho, (a, x), r - 2, STRIP) + at(rho, (a, x), r + 2, STRIP)
                for n in apart:
                    far = far + at(rho, (a, n), r, STRIP)
                side = at(s_ref, s_idx, r - 1, STRIP) + at(s_ref, s_idx, r + 1, STRIP)
                split(left, a, rows, nz, c + (2.0 * beta) * q)
                left[a, rows, 2 * nz:] = c.astype(bf)
                base[a, rows, :] = (kappa * c + q) + beta * (far + (side + side))

    def finish(x):
        left, base = lefts[x % 2], bases[x % 2]
        mixed = [jnp.dot(left[a], mix[...], preferred_element_type=f32) for a in range(na)]
        for i in range(steps):
            rows = slice(i * STRIP, (i + 1) * STRIP)
            total = None
            for a in range(na):
                w = at(p, (a, x), i * STRIP, STRIP).astype(f32) * (base[a, rows, :] + mixed[a][rows])
                total = w if total is None else total + w
            e[0, x, rows, :] = total * (-g1)

    prepare(0)
    for x in range(1, nx):
        prepare(x)
        finish(x - 1)
    finish(nx - 1)


def inner(o, p):
    nj, nx, ny, nz = o.shape
    na = p.shape[0]
    g = polynomial()
    f32, bf = jnp.float32, jnp.bfloat16
    mix = mixing(nz, g[2] / g[1])
    return pl.pallas_call(
        inner_kernel,
        grid=(nj,),
        out_shape=jax.ShapeDtypeStruct((nj, nx, ny, nz), f32),
        in_specs=[
            pl.BlockSpec((1, nx, ny, nz), lambda j: (j, 0, 0, 0)),
            pl.BlockSpec((na, nx, ny, nz), lambda j: (0, 0, 0, 0)),
            pl.BlockSpec(mix.shape, lambda j: (0, 0)),
        ],
        out_specs=pl.BlockSpec((1, nx, ny, nz), lambda j: (j, 0, 0, 0)),
        scratch_shapes=[pltpu.VMEM((na, nx, ny + 2 * PAD, nz), f32)]
        + [pltpu.VMEM((na, ny + 2 * PAD, nz), f32)] * 2
        + [pltpu.VMEM((na, ny, 3 * nz), bf)] * 2
        + [pltpu.VMEM((na, ny, nz), f32)] * 2,
        compiler_params=pltpu.CompilerParams(vmem_limit_bytes=40 * 2**20),
        cost_estimate=pl.CostEstimate(flops=6 * 10**9, bytes_accessed=8 * 2**20, transcendentals=0),
        name="inner_field",
    )(o, p, mix)


def outer_kernel(e_in, o, near_low, far_low, near_high, far_high, p, plo, phi, mix, e, ace, *scratch):
    g0, g1, g2 = polynomial()
    beta = g2 / g1
    na, nx, ny, nz = p.shape
    nj = o.shape[0]
    steps = ny // STRIP
    f32, bf = jnp.float32, jnp.bfloat16
    rhos, lefts, bases = scratch[0:2], scratch[2:4], scratch[4:6]
    sides = ((0, near_low, far_low, plo, 1, 0, 0, 1), (1, near_high, far_high, phi, 0, 1, nx - 1, nx - 2))

    def prepare(s, near, far, ph, h1, h2, t0, t1):
        rho, left, base = rhos[s], lefts[s], bases[s]
        for i in range(steps):
            ov = at(near, (0, 0), i * STRIP, STRIP).astype(f32)
            for a in range(na):
                rho[a, PAD + i * STRIP:PAD + (i + 1) * STRIP, :] = at(ph, (a, h1), i * STRIP, STRIP).astype(f32) * ov
        for a in range(na):
            wrap(rho, (a,), ny, 1)
        for i in range(steps):
            r = PAD + i * STRIP
            rows = slice(i * STRIP, (i + 1) * STRIP)
            ov = at(far, (0, 0), i * STRIP, STRIP).astype(f32)
            step = None
            for a in range(na):
                c = at(rho, (a,), r, STRIP)
                split(left, a, rows, nz, c)
                y = at(rho, (a,), r - 1, STRIP) + at(rho, (a,), r + 1, STRIP)
                base[a, rows, :] = (c + beta * (at(ph, (a, h2), i * STRIP, STRIP).astype(f32) * ov)) + (2.0 * beta) * y
                w = at(p, (a, t1), i * STRIP, STRIP).astype(f32) * c
                step = w if step is None else step + w
            e[0, t1, rows, :] = at(e_in, (0, t1), i * STRIP, STRIP) + step * (-g1 * beta)

    def finish(s, near, far, ph, h1, h2, t0, t1):
        left, base = lefts[s], bases[s]
        mixed = [jnp.dot(left[a], mix[:2 * nz, :], preferred_element_type=f32) for a in range(na)]
        for i in range(steps):
            rows = slice(i * STRIP, (i + 1) * STRIP)
            step = None
            for a in range(na):
                w = at(p, (a, t0), i * STRIP, STRIP).astype(f32) * (base[a, rows, :] + (2.0 * beta) * mixed[a][rows])
                step = w if step is None else step + w
            e[0, t0, rows, :] = at(e_in, (0, t0), i * STRIP, STRIP) + step * (-g1)

    prepare(*sides[0])
    prepare(*sides[1])
    finish(*sides[0])
    finish(*sides[1])

    def project(x, acc):
        acc = list(acc)
        for i in range(steps):
            field = at(e, (0, x), i * STRIP, STRIP)
            for s in range(na + nj):
                source = at(p, (s, x), i * STRIP, STRIP) if s < na else at(o, (s - na, x), i * STRIP, STRIP)
                m = source.astype(f32) * field
                m = m[:, :128] + m[:, 128:]
                acc[s] = acc[s] + jnp.sum(m.reshape(STRIP // 8, 8, 128), axis=0)
        return tuple(acc)

    acc = lax.fori_loop(0, nx, project, tuple(jnp.zeros((8, 128), f32) for _ in range(na + nj)))
    for s in range(na + nj):
        part = jnp.sum(jnp.sum(acc[s], axis=0, keepdims=True), axis=1, keepdims=True)
        ace[0, s:s + 1, :] = jnp.broadcast_to(part, (1, 128))


def outer(e, o, halo, p, plo, phi):
    nj, nx, ny, nz = o.shape
    na = p.shape[0]
    g = polynomial()
    f32, bf = jnp.float32, jnp.bfloat16
    mix = mixing(nz, g[2] / g[1])
    each = lambda shape: pl.BlockSpec((1, *shape[1:]), lambda j: (j, *(0,) * (len(shape) - 1)))
    whole = lambda shape: pl.BlockSpec(shape, lambda j: (0,) * len(shape))
    return pl.pallas_call(
        outer_kernel,
        grid=(nj,),
        out_shape=(jax.ShapeDtypeStruct(e.shape, f32), jax.ShapeDtypeStruct((nj, 8, 128), f32)),
        in_specs=[each(e.shape), whole(o.shape), *[each(h.shape) for h in halo], whole(p.shape), whole(plo.shape), whole(phi.shape), whole(mix.shape)],
        out_specs=(each(e.shape), each((nj, 8, 128))),
        input_output_aliases={0: 0},
        scratch_shapes=[pltpu.VMEM((na, ny + 2 * PAD, nz), f32)] * 2
        + [pltpu.VMEM((na, ny, 2 * nz), bf)] * 2
        + [pltpu.VMEM((na, ny, nz), f32)] * 2,
        compiler_params=pltpu.CompilerParams(vmem_limit_bytes=40 * 2**20),
        cost_estimate=pl.CostEstimate(flops=3 * 10**9, bytes_accessed=14 * 2**20, transcendentals=0),
        name="outer_field",
    )(e, o, *halo, p, plo, phi, mix)


def cut_kernel(row, orbitals, *refs):
    parts = refs[:PANEL * row]
    held, loaded, stored = refs[PANEL * row:]
    x = lax.rem(lax.axis_index("band"), row)
    loads = [pltpu.make_async_copy(orbitals.at[a], held.at[a], loaded.at[a]) for a in range(PANEL)]
    stores = [
        pltpu.make_async_copy(held.at[a, lax.rem(x + k, row)], parts[a * row + k], stored.at[a * row + k])
        for a in range(PANEL)
        for k in range(row)
    ]
    for a in range(PANEL):
        loads[a].start()
    for a in range(PANEL):
        loads[a].wait()
        for k in range(row):
            stores[a * row + k].start()
    for c in stores:
        c.wait()


def cut(orbitals):
    row, ny, nz = orbitals.shape[1:]
    part = jax.ShapeDtypeStruct((ny, nz), orbitals.dtype)
    anywhere = pl.BlockSpec(memory_space=pl.ANY)
    parts = pl.pallas_call(
        lambda *refs: cut_kernel(row, *refs),
        out_shape=(part,) * (PANEL * row),
        in_specs=[anywhere],
        out_specs=(anywhere,) * (PANEL * row),
        scratch_shapes=[
            pltpu.VMEM((PANEL, row, ny, nz), orbitals.dtype),
            pltpu.SemaphoreType.DMA((PANEL,)),
            pltpu.SemaphoreType.DMA((PANEL * row,)),
        ],
        name="cut_panel",
    )(orbitals)
    return [parts[a * row:(a + 1) * row] for a in range(PANEL)]


def join_kernel(row, *refs):
    parts, (panel, top, bottom), (held, loaded, stored) = refs[:PANEL * row], refs[PANEL * row:-3], refs[-3:]
    x = lax.rem(lax.axis_index("band"), row)
    loads = [
        pltpu.make_async_copy(parts[a * row + k], held.at[a, lax.rem(x + row - k, row)], loaded.at[a * row + k])
        for a in range(PANEL)
        for k in range(row)
    ]
    stores = [
        pltpu.make_async_copy(held.at[:, row - 2:], top, stored.at[0]),
        pltpu.make_async_copy(held.at[:, :2], bottom, stored.at[1]),
        pltpu.make_async_copy(held, panel, stored.at[2]),
    ]
    for c in loads:
        c.start()
    for c in loads:
        c.wait()
    for c in stores:
        c.start()
    for c in stores:
        c.wait()


def join(parts):
    row = len(parts) // PANEL
    ny, nz = parts[0].shape
    dtype = parts[0].dtype
    anywhere = pl.BlockSpec(memory_space=pl.ANY)
    edge = jax.ShapeDtypeStruct((PANEL, 2, ny, nz), dtype)
    return pl.pallas_call(
        lambda *refs: join_kernel(row, *refs),
        out_shape=(jax.ShapeDtypeStruct((PANEL, row, ny, nz), dtype), edge, edge),
        in_specs=[anywhere] * (PANEL * row),
        out_specs=(anywhere,) * 3,
        scratch_shapes=[
            pltpu.VMEM((PANEL, row, ny, nz), dtype),
            pltpu.SemaphoreType.DMA((PANEL * row,)),
            pltpu.SemaphoreType.DMA((3,)),
        ],
        name="join_panel",
    )(*parts)


def ring(count, shift):
    return [(i, (i + shift) % count) for i in range(count)]


def rows(shift, row):
    count = lax.axis_size("band")
    return [(i, i // row * row + (i + shift) % row) for i in range(count)]


def total(part):
    count = lax.axis_size("dom")
    for group in ((1,), (2,), (4, 8, 12)):
        moved = [lax.ppermute(part, "dom", [(i, i ^ k) for i in range(count)]) for k in group]
        for m in moved:
            part = part + m
    return part


def local(orbitals, owner_band):
    nj, nx, ny, nz = orbitals.shape
    row = nx
    me = lax.axis_index("band")
    owner = owner_band[0]
    behind = lax.rem(me + row - lax.rem(owner, row), row)
    same = lax.div(me, row) == lax.div(owner, row)
    up = lambda v: lax.ppermute(v, "dom", ring(lax.axis_size("dom"), 1))
    down = lambda v: lax.ppermute(v, "dom", ring(lax.axis_size("dom"), -1))
    along = lambda v, k: lax.ppermute(v, "band", rows(k, row))
    across = lambda v: lax.ppermute(v, "band", ring(lax.axis_size("band"), row))
    plane = lambda v, x: v[:, x:x + 1]

    pieces = cut(orbitals)
    got = [[pieces[a][0]] + [along(pieces[a][k], k) for k in range(1, row)] for a in range(PANEL)]
    mine = [lax.select_n(behind, *g) for g in got]
    mine[0], *near = lax.optimization_barrier((mine[0], plane(orbitals, nx - 1), plane(orbitals, 0)))
    near = (up(near[0]), down(near[1]))
    mine = [jnp.where(same, m, across(m)) for m in mine]
    parts = [[m, *[along(m, k) for k in range(1, row)]] for m in mine]
    *parts[0], near_low, near_high, far_low, far_high = lax.optimization_barrier(
        (*parts[0], *near, plane(orbitals, nx - 2), plane(orbitals, 1)))
    near, far = (near_low, near_high), (up(far_low), down(far_high))
    panel, top, bottom = join(parts[0] + parts[1])
    low, high = up(top), down(bottom)
    exchange = inner(orbitals, panel)
    exchange, sums = outer(exchange, orbitals, (near[0], far[0], near[1], far[1]), panel, low, high)
    cells = float(nx * lax.axis_size("dom") * ny * nz)
    ace_block = jnp.transpose(total(sums)[:, :PANEL + nj, 0]) / cells
    return exchange, ace_block[None]


def solution(mesh):
    placed = (P("band", "dom", None, None), P())
    return jax.shard_map(
        local,
        mesh=mesh,
        in_specs=placed,
        out_specs=(P("band", "dom", None, None), P("band", None, None)),
        check_vma=False,
    )
```

```python
import math

import jax
import jax.numpy as jnp
import numpy as np
from jax import lax
from jax.experimental import pallas as pl
from jax.experimental.pallas import tpu as pltpu
from jax.sharding import PartitionSpec as P

PANEL, SWEEPS, SCREEN = 2, 3, 0.1
PAD = 8
STRIP = 32


def polynomial():
    d = 6.0 + SCREEN
    w = [1.0 / (1.0 + 6.0 / d * math.cos(math.pi * (2 * k + 1) / (2 * SWEEPS))) for k in range(SWEEPS)]
    p = [w[0] / d]
    for k in range(1, SWEEPS):
        n = [0.0] * (len(p) + 1)
        for i, c in enumerate(p):
            n[i] += c * (1.0 - w[k])
            n[i + 1] += c * w[k] / d
        n[0] += w[k] / d
        p = n
    return p


def mixing(nz, beta):
    near = np.zeros((nz, nz), np.float32)
    far = np.zeros((nz, nz), np.float32)
    for z in range(nz):
        for s, m in ((1, near), (2, far)):
            m[(z - s) % nz, z] += 1.0
            m[(z + s) % nz, z] += 1.0
    return jnp.asarray(np.concatenate([near, near, beta * far], 0)).astype(jnp.bfloat16)


LANES = 128


def at(ref, idx, start, size, h):
    return ref[(*idx, slice(start, start + size), slice(h * LANES, (h + 1) * LANES))]


def sp(ref, idx, start, size, h):
    return ref[(*idx, h, slice(start, start + size), slice(None))]


def wrap(ref, idx, halves, ny, width):
    for h in range(halves):
        ref[(*idx, h, slice(PAD - width, PAD), slice(None))] = sp(ref, idx, PAD + ny - width, width, h)
        ref[(*idx, h, slice(PAD + ny, PAD + ny + width), slice(None))] = sp(ref, idx, PAD, width, h)


def split(left, rows, nz, h, v):
    hi = v.astype(jnp.bfloat16)
    left[rows, h * LANES:(h + 1) * LANES] = hi
    left[rows, nz + h * LANES:nz + (h + 1) * LANES] = (v - hi.astype(jnp.float32)).astype(jnp.bfloat16)


def inner_kernel(o, p, mix, e, rho, *scratch):
    g0, g1, g2 = polynomial()
    beta = g2 / g1
    kappa = g0 / g1 + 6.0 * beta
    na, nx, ny, nz = p.shape
    steps, halves = ny // STRIP, nz // LANES
    f32, bf = jnp.float32, jnp.bfloat16
    sigs, lefts, bases = scratch[0:2], scratch[2:4], scratch[4:6]

    for x in range(nx):
        for i in range(steps):
            for h in range(halves):
                ov = at(o, (0, x), i * STRIP, STRIP, h).astype(f32)
                for a in range(na):
                    rho[a, x, h, PAD + i * STRIP:PAD + (i + 1) * STRIP, :] = at(p, (a, x), i * STRIP, STRIP, h).astype(f32) * ov
        for a in range(na):
            wrap(rho, (a, x), halves, ny, 2)

    def prepare(x):
        sig, left, base = sigs[x % 2], lefts[x % 2], bases[x % 2]
        near = [n for n in (x - 1, x + 1) if 0 <= n < nx]
        apart = [n for n in (x - 2, x + 2) if 0 <= n < nx]
        if len(near) > 1:
            for a in range(na):
                for h in range(halves):
                    for r in range(0, ny + 2 * PAD, 16):
                        sig[a, h, r:r + 16, :] = sp(rho, (a, near[0]), r, 16, h) + sp(rho, (a, near[1]), r, 16, h)
        for a in range(na):
            s_ref, s_idx = (sig, (a,)) if len(near) > 1 else (rho, (a, near[0]))
            for i in range(steps):
                for h in range(halves):
                    r = PAD + i * STRIP
                    rows = slice(i * STRIP, (i + 1) * STRIP)
                    c = sp(rho, (a, x), r, STRIP, h)
                    q = sp(s_ref, s_idx, r, STRIP, h) + (sp(rho, (a, x), r - 1, STRIP, h) + sp(rho, (a, x), r + 1, STRIP, h))
                    far = sp(rho, (a, x), r - 2, STRIP, h) + sp(rho, (a, x), r + 2, STRIP, h)
                    for n in apart:
                        far = far + sp(rho, (a, n), r, STRIP, h)
                    side = sp(s_ref, s_idx, r - 1, STRIP, h) + sp(s_ref, s_idx, r + 1, STRIP, h)
                    split(left.at[a], rows, nz, h, c + (2.0 * beta) * q)
                    left[a, rows, 2 * nz + h * LANES:2 * nz + (h + 1) * LANES] = c.astype(bf)
                    base[a, rows, h * LANES:(h + 1) * LANES] = (kappa * c + q) + beta * (far + (side + side))

    def finish(x):
        left, base = lefts[x % 2], bases[x % 2]
        mixed = [jnp.dot(left[a], mix[...], preferred_element_type=f32) for a in range(na)]
        for i in range(steps):
            rows = slice(i * STRIP, (i + 1) * STRIP)
            total = None
            for a in range(na):
                w = p[a, x, rows, :].astype(f32) * (base[a, rows, :] + mixed[a][rows])
                total = w if total is None else total + w
            e[pl.program_id(0), x, rows, :] = total * (-g1)

    prepare(0)
    for x in range(1, nx):
        prepare(x)
        finish(x - 1)
    finish(nx - 1)


def inner(o, p):
    nj, nx, ny, nz = o.shape
    na = p.shape[0]
    g = polynomial()
    f32, bf = jnp.float32, jnp.bfloat16
    mix = mixing(nz, g[2] / g[1])
    return pl.pallas_call(
        inner_kernel,
        grid=(nj,),
        out_shape=pltpu.VMEM((nj, nx, ny, nz), f32),
        in_specs=[
            pl.BlockSpec((1, nx, ny, nz), lambda j: (j, 0, 0, 0)),
            pl.BlockSpec(memory_space=pltpu.VMEM),
            pl.BlockSpec(mix.shape, lambda j: (0, 0)),
        ],
        out_specs=pl.BlockSpec(memory_space=pltpu.VMEM),
        scratch_shapes=[pltpu.VMEM((na, nx, nz // LANES, ny + 2 * PAD, LANES), f32)]
        + [pltpu.VMEM((na, nz // LANES, ny + 2 * PAD, LANES), f32)] * 2
        + [pltpu.VMEM((na, ny, 3 * nz), bf)] * 2
        + [pltpu.VMEM((na, ny, nz), f32)] * 2,
        compiler_params=pltpu.CompilerParams(vmem_limit_bytes=20 * 2**20),
        cost_estimate=pl.CostEstimate(flops=6 * 10**9, bytes_accessed=8 * 2**20, transcendentals=0),
        name="inner_field",
    )(o, p, mix)


def outer_kernel(e_in, o, halo_low, halo_high, p, plo, phi, mix, e, ace, *scratch):
    g0, g1, g2 = polynomial()
    beta = g2 / g1
    na, nx, ny, nz = p.shape
    nj = o.shape[0]
    steps, halves = ny // STRIP, nz // LANES
    f32, bf = jnp.float32, jnp.bfloat16
    rhos, lefts, bases = scratch[0:2], scratch[2:4], scratch[4:6]
    sides = ((0, halo_low, plo, 1, 0, 0, 1), (1, halo_high, phi, 0, 1, nx - 1, nx - 2))

    def prepare(s, halo, ph, h1, h2, t0, t1):
        rho, left, base = rhos[s], lefts[s], bases[s]
        for i in range(steps):
            for h in range(halves):
                ov = at(halo, (0, h1), i * STRIP, STRIP, h).astype(f32)
                for a in range(na):
                    rho[a, h, PAD + i * STRIP:PAD + (i + 1) * STRIP, :] = at(ph, (a, h1), i * STRIP, STRIP, h).astype(f32) * ov
        for a in range(na):
            wrap(rho, (a,), halves, ny, 1)
        for i in range(steps):
            for h in range(halves):
                r = PAD + i * STRIP
                rows = slice(i * STRIP, (i + 1) * STRIP)
                lanes = slice(h * LANES, (h + 1) * LANES)
                ov = at(halo, (0, h2), i * STRIP, STRIP, h).astype(f32)
                step = None
                for a in range(na):
                    c = sp(rho, (a,), r, STRIP, h)
                    split(left.at[a], rows, nz, h, c)
                    y = sp(rho, (a,), r - 1, STRIP, h) + sp(rho, (a,), r + 1, STRIP, h)
                    base[a, rows, lanes] = (c + beta * (at(ph, (a, h2), i * STRIP, STRIP, h).astype(f32) * ov)) + (2.0 * beta) * y
                    w = at(p, (a, t1), i * STRIP, STRIP, h).astype(f32) * c
                    step = w if step is None else step + w
                e[0, t1, rows, lanes] = at(e_in, (pl.program_id(0), t1), i * STRIP, STRIP, h) + step * (-g1 * beta)

    def finish(s, halo, ph, h1, h2, t0, t1):
        left, base = lefts[s], bases[s]
        mixed = [jnp.dot(left[a], mix[:2 * nz, :], preferred_element_type=f32) for a in range(na)]
        for i in range(steps):
            rows = slice(i * STRIP, (i + 1) * STRIP)
            step = None
            for a in range(na):
                w = p[a, t0, rows, :].astype(f32) * (base[a, rows, :] + (2.0 * beta) * mixed[a][rows])
                step = w if step is None else step + w
            e[0, t0, rows, :] = e_in[pl.program_id(0), t0, rows, :] + step * (-g1)

    prepare(*sides[0])
    prepare(*sides[1])
    finish(*sides[0])
    finish(*sides[1])

    def project(x, acc):
        acc = list(acc)
        for i in range(steps):
            rows = slice(i * STRIP, (i + 1) * STRIP)
            field = e[0, x, rows, :]
            for s in range(na + nj):
                source = p[s, x, rows, :] if s < na else o[s - na, x, rows, :]
                m = source.astype(f32) * field
                m = m[:, :128] + m[:, 128:]
                acc[s] = acc[s] + jnp.sum(m.reshape(STRIP // 8, 8, 128), axis=0)
        return tuple(acc)

    acc = lax.fori_loop(0, nx, project, tuple(jnp.zeros((8, 128), f32) for _ in range(na + nj)))
    sums = [jnp.sum(a, axis=0, keepdims=True) for a in acc]
    tile = jnp.concatenate(sums + [jnp.zeros((8 - na - nj, LANES), f32)], axis=0)
    share = LANES // nj
    width = LANES // 2
    while width >= share:
        tile = tile + pltpu.roll(tile, width, 1)
        width //= 2
    j = pl.program_id(0)
    lane = lax.broadcasted_iota(jnp.int32, (8, LANES), 1)
    tile = jnp.where((lane >= j * share) & (lane < (j + 1) * share), tile, jnp.where(j == 0, 0.0, ace[...]))
    ace[...] = tile


def outer(e, o, halo, p, plo, phi):
    nj, nx, ny, nz = o.shape
    na = p.shape[0]
    g = polynomial()
    f32, bf = jnp.float32, jnp.bfloat16
    mix = mixing(nz, g[2] / g[1])
    each = lambda shape: pl.BlockSpec((1, *shape[1:]), lambda j: (j, *(0,) * (len(shape) - 1)))
    whole = lambda shape: pl.BlockSpec(shape, lambda j: (0,) * len(shape))
    return pl.pallas_call(
        outer_kernel,
        grid=(nj,),
        out_shape=(jax.ShapeDtypeStruct(e.shape, f32), jax.ShapeDtypeStruct((8, LANES), f32)),
        in_specs=[pl.BlockSpec(memory_space=pltpu.VMEM), whole(o.shape), *[each(h.shape) for h in halo], pl.BlockSpec(memory_space=pltpu.VMEM), whole(plo.shape), whole(phi.shape), whole(mix.shape)],
        out_specs=(each(e.shape), pl.BlockSpec((8, LANES), lambda j: (0, 0))),
        scratch_shapes=[pltpu.VMEM((na, nz // LANES, ny + 2 * PAD, LANES), f32)] * 2
        + [pltpu.VMEM((na, ny, 2 * nz), bf)] * 2
        + [pltpu.VMEM((na, ny, nz), f32)] * 2,
        compiler_params=pltpu.CompilerParams(vmem_limit_bytes=24 * 2**20),
        cost_estimate=pl.CostEstimate(flops=3 * 10**9, bytes_accessed=14 * 2**20, transcendentals=0),
        name="outer_field",
    )(e, o, *halo, p, plo, phi, mix)


def cut_kernel(row, orbitals, *refs):
    parts = refs[:PANEL * row]
    held, loaded, stored = refs[PANEL * row:]
    x = lax.rem(lax.axis_index("band"), row)
    loads = [pltpu.make_async_copy(orbitals.at[a], held.at[a], loaded.at[a]) for a in range(PANEL)]
    stores = [
        pltpu.make_async_copy(held.at[a, lax.rem(x + k, row)], parts[a * row + k], stored.at[a * row + k])
        for a in range(PANEL)
        for k in range(row)
    ]
    for a in range(PANEL):
        loads[a].start()
    for a in range(PANEL):
        loads[a].wait()
        for k in range(row):
            stores[a * row + k].start()
    for c in stores:
        c.wait()


def cut(orbitals):
    row, ny, nz = orbitals.shape[1:]
    part = jax.ShapeDtypeStruct((ny, nz), orbitals.dtype)
    hbm = pl.BlockSpec(memory_space=pltpu.HBM)
    parts = pl.pallas_call(
        lambda *refs: cut_kernel(row, *refs),
        out_shape=(part,) * (PANEL * row),
        in_specs=[hbm],
        out_specs=(hbm,) * (PANEL * row),
        scratch_shapes=[
            pltpu.VMEM((PANEL, row, ny, nz), orbitals.dtype),
            pltpu.SemaphoreType.DMA((PANEL,)),
            pltpu.SemaphoreType.DMA((PANEL * row,)),
        ],
        name="cut_panel",
    )(orbitals)
    return [parts[a * row:(a + 1) * row] for a in range(PANEL)]


def edges_kernel(orbitals, top, bottom, held, loaded, stored):
    nx = orbitals.shape[1]
    loads = [pltpu.make_async_copy(orbitals.at[:, a:a + 2], held.at[n], loaded.at[n]) for n, a in enumerate((nx - 2, 0))]
    stores = [pltpu.make_async_copy(held.at[n], out, stored.at[n]) for n, out in enumerate((top, bottom))]
    for c in loads:
        c.start()
    for load, store in zip(loads, stores):
        load.wait()
        store.start()
    for c in stores:
        c.wait()


def edges(orbitals):
    nj, _, ny, nz = orbitals.shape
    hbm = pl.BlockSpec(memory_space=pltpu.HBM)
    return pl.pallas_call(
        edges_kernel,
        out_shape=(jax.ShapeDtypeStruct((nj, 2, ny, nz), orbitals.dtype),) * 2,
        in_specs=[hbm],
        out_specs=(hbm, hbm),
        scratch_shapes=[pltpu.VMEM((2, nj, 2, ny, nz), orbitals.dtype), pltpu.SemaphoreType.DMA((2,)), pltpu.SemaphoreType.DMA((2,))],
        name="edge_planes",
    )(orbitals)


def join_kernel(row, *refs):
    parts, (panel, top, bottom, loaded, stored) = refs[:PANEL * row], refs[PANEL * row:]
    x = lax.rem(lax.axis_index("band"), row)
    loads = [
        pltpu.make_async_copy(parts[a * row + k], panel.at[a, lax.rem(x + row - k, row)], loaded.at[a * row + k])
        for a in range(PANEL)
        for k in range(row)
    ]
    stores = [
        pltpu.make_async_copy(panel.at[:, row - 2:], top, stored.at[0]),
        pltpu.make_async_copy(panel.at[:, :2], bottom, stored.at[1]),
    ]
    for c in loads:
        c.start()
    for c in loads:
        c.wait()
    for c in stores:
        c.start()
    for c in stores:
        c.wait()


def join(parts):
    row = len(parts) // PANEL
    ny, nz = parts[0].shape
    dtype = parts[0].dtype
    hbm = pl.BlockSpec(memory_space=pl.ANY)
    edge = pltpu.VMEM((PANEL, 2, ny, nz), dtype)
    return pl.pallas_call(
        lambda *refs: join_kernel(row, *refs),
        out_shape=(pltpu.VMEM((PANEL, row, ny, nz), dtype), edge, edge),
        in_specs=[hbm] * (PANEL * row),
        out_specs=(pl.BlockSpec(memory_space=pltpu.VMEM),) * 3,
        scratch_shapes=[pltpu.SemaphoreType.DMA((PANEL * row,)), pltpu.SemaphoreType.DMA((2,))],
        name="join_panel",
    )(*parts)


def ring(count, shift):
    return [(i, (i + shift) % count) for i in range(count)]


def rows(shift, row):
    count = lax.axis_size("band")
    return [(i, i // row * row + (i + shift) % row) for i in range(count)]


def total(part):
    count = lax.axis_size("dom")
    for group in ((1,), (2,), (4, 8, 12)):
        moved = [lax.ppermute(part, "dom", [(i, i ^ k) for i in range(count)]) for k in group]
        for m in moved:
            part = part + m
    return part


def local(orbitals, owner_band):
    nj, nx, ny, nz = orbitals.shape
    row = nx
    slabs = lax.axis_size("dom")
    me = lax.axis_index("band")
    owner = owner_band[0]
    behind = lax.rem(me + row - lax.rem(owner, row), row)
    same = lax.div(me, row) == lax.div(owner, row)
    up = lambda v: lax.ppermute(v, "dom", ring(lax.axis_size("dom"), 1))
    down = lambda v: lax.ppermute(v, "dom", ring(lax.axis_size("dom"), -1))
    along = lambda v, k: lax.ppermute(v, "band", rows(k, row))
    across = lambda v: lax.ppermute(v, "band", ring(lax.axis_size("band"), row))

    pieces = cut(orbitals)
    o_top, o_bottom = edges(orbitals)
    got = [[pieces[n][0]] + [along(pieces[n][m], m) for m in range(1, row)] for n in range(PANEL)]
    mine = [lax.select_n(behind, *g) for g in got]
    mine[0], o_top, o_bottom = lax.optimization_barrier((mine[0], o_top, o_bottom))
    halo = (up(o_top), down(o_bottom))
    mine = [jnp.where(same, m, across(m)) for m in mine]
    parts = [[m, *[along(m, n) for n in range(1, row)]] for m in mine]
    panel, top, bottom = join(parts[0] + parts[1])
    low, high = up(top), down(bottom)
    exchange = inner(orbitals, panel)
    exchange, sums = outer(exchange, orbitals, halo, panel, low, high)
    cells = float(nx * slabs * ny * nz)
    ace_block = jnp.sum(total(sums)[:PANEL + nj].reshape(PANEL + nj, nj, -1), axis=2) / cells
    return exchange, ace_block[None]


def solution(mesh):
    placed = (P("band", "dom", None, None), P())
    return jax.shard_map(
        local,
        mesh=mesh,
        in_specs=placed,
        out_specs=(P("band", "dom", None, None), P("band", None, None)),
        check_vma=False,
    )
```

```python
import math

import jax
import jax.numpy as jnp
import numpy as np
from jax import lax
from jax.experimental import pallas as pl
from jax.experimental.pallas import tpu as pltpu
from jax.sharding import PartitionSpec as P

PANEL, SWEEPS, SCREEN = 2, 3, 0.1
PAD = 8
STRIP = 32


def polynomial():
    d = 6.0 + SCREEN
    w = [1.0 / (1.0 + 6.0 / d * math.cos(math.pi * (2 * k + 1) / (2 * SWEEPS))) for k in range(SWEEPS)]
    p = [w[0] / d]
    for k in range(1, SWEEPS):
        n = [0.0] * (len(p) + 1)
        for i, c in enumerate(p):
            n[i] += c * (1.0 - w[k])
            n[i + 1] += c * w[k] / d
        n[0] += w[k] / d
        p = n
    return p


def mixing(nz, beta):
    near = np.zeros((nz, nz), np.float32)
    far = np.zeros((nz, nz), np.float32)
    for z in range(nz):
        for s, m in ((1, near), (2, far)):
            m[(z - s) % nz, z] += 1.0
            m[(z + s) % nz, z] += 1.0
    return jnp.asarray(np.concatenate([near, near, beta * far], 0)).astype(jnp.bfloat16)


LANES = 128


def at(ref, idx, start, size, h):
    return ref[(*idx, slice(start, start + size), slice(h * LANES, (h + 1) * LANES))]


def sp(ref, idx, start, size, h):
    return ref[(*idx, h, slice(start, start + size), slice(None))]


def wrap(ref, idx, halves, ny, width):
    for h in range(halves):
        ref[(*idx, h, slice(PAD - width, PAD), slice(None))] = sp(ref, idx, PAD + ny - width, width, h)
        ref[(*idx, h, slice(PAD + ny, PAD + ny + width), slice(None))] = sp(ref, idx, PAD, width, h)


def split(left, rows, nz, h, v):
    hi = v.astype(jnp.bfloat16)
    left[rows, h * LANES:(h + 1) * LANES] = hi
    left[rows, nz + h * LANES:nz + (h + 1) * LANES] = (v - hi.astype(jnp.float32)).astype(jnp.bfloat16)


def inner_kernel(o, p, mix, e, o_wide, p_wide, rho, *scratch):
    j = pl.program_id(0)
    g0, g1, g2 = polynomial()
    beta = g2 / g1
    kappa = g0 / g1 + 6.0 * beta
    na, nx, ny, nz = p.shape
    steps, halves = ny // STRIP, nz // LANES
    f32, bf = jnp.float32, jnp.bfloat16
    sigs, lefts, bases = scratch[0:2], scratch[2:4], scratch[4:6]

    for x in range(nx):
        for i in range(steps):
            for h in range(halves):
                ov = at(o, (0, x), i * STRIP, STRIP, h).astype(f32)
                o_wide[j, x, i * STRIP:(i + 1) * STRIP, h * LANES:(h + 1) * LANES] = ov
                for a in range(na):
                    rho[a, x, h, PAD + i * STRIP:PAD + (i + 1) * STRIP, :] = at(p, (a, x), i * STRIP, STRIP, h).astype(f32) * ov
        for a in range(na):
            wrap(rho, (a, x), halves, ny, 2)

    @pl.when(j == 0)
    def _():
        for a in range(na):
            for x in range(nx):
                for i in range(steps):
                    rows = slice(i * STRIP, (i + 1) * STRIP)
                    p_wide[a, x, rows, :] = p[a, x, rows, :].astype(f32)

    def prepare(x):
        sig, left, base = sigs[x % 2], lefts[x % 2], bases[x % 2]
        near = [n for n in (x - 1, x + 1) if 0 <= n < nx]
        apart = [n for n in (x - 2, x + 2) if 0 <= n < nx]
        if len(near) > 1:
            for a in range(na):
                for h in range(halves):
                    for r in range(0, ny + 2 * PAD, 16):
                        sig[a, h, r:r + 16, :] = sp(rho, (a, near[0]), r, 16, h) + sp(rho, (a, near[1]), r, 16, h)
        for a in range(na):
            s_ref, s_idx = (sig, (a,)) if len(near) > 1 else (rho, (a, near[0]))
            for i in range(steps):
                for h in range(halves):
                    r = PAD + i * STRIP
                    rows = slice(i * STRIP, (i + 1) * STRIP)
                    c = sp(rho, (a, x), r, STRIP, h)
                    q = sp(s_ref, s_idx, r, STRIP, h) + (sp(rho, (a, x), r - 1, STRIP, h) + sp(rho, (a, x), r + 1, STRIP, h))
                    far = sp(rho, (a, x), r - 2, STRIP, h) + sp(rho, (a, x), r + 2, STRIP, h)
                    for n in apart:
                        far = far + sp(rho, (a, n), r, STRIP, h)
                    side = sp(s_ref, s_idx, r - 1, STRIP, h) + sp(s_ref, s_idx, r + 1, STRIP, h)
                    split(left.at[a], rows, nz, h, c + (2.0 * beta) * q)
                    left[a, rows, 2 * nz + h * LANES:2 * nz + (h + 1) * LANES] = c.astype(bf)
                    base[a, rows, h * LANES:(h + 1) * LANES] = (kappa * c + q) + beta * (far + (side + side))

    def finish(x):
        left, base = lefts[x % 2], bases[x % 2]
        mixed = [jnp.dot(left[a], mix[...], preferred_element_type=f32) for a in range(na)]
        for i in range(steps):
            rows = slice(i * STRIP, (i + 1) * STRIP)
            total = None
            for a in range(na):
                w = p[a, x, rows, :].astype(f32) * (base[a, rows, :] + mixed[a][rows])
                total = w if total is None else total + w
            e[pl.program_id(0), x, rows, :] = total * (-g1)

    prepare(0)
    for x in range(1, nx):
        prepare(x)
        finish(x - 1)
    finish(nx - 1)


def inner(o, p):
    nj, nx, ny, nz = o.shape
    na = p.shape[0]
    g = polynomial()
    f32, bf = jnp.float32, jnp.bfloat16
    mix = mixing(nz, g[2] / g[1])
    return pl.pallas_call(
        inner_kernel,
        grid=(nj,),
        out_shape=(pltpu.VMEM((nj, nx, ny, nz), f32), pltpu.VMEM((nj, nx, ny, nz), f32), pltpu.VMEM((na, nx, ny, nz), f32)),
        in_specs=[
            pl.BlockSpec((1, nx, ny, nz), lambda j: (j, 0, 0, 0)),
            pl.BlockSpec(memory_space=pltpu.VMEM),
            pl.BlockSpec(mix.shape, lambda j: (0, 0)),
        ],
        out_specs=(pl.BlockSpec(memory_space=pltpu.VMEM),) * 3,
        scratch_shapes=[pltpu.VMEM((na, nx, nz // LANES, ny + 2 * PAD, LANES), f32)]
        + [pltpu.VMEM((na, nz // LANES, ny + 2 * PAD, LANES), f32)] * 2
        + [pltpu.VMEM((na, ny, 3 * nz), bf)] * 2
        + [pltpu.VMEM((na, ny, nz), f32)] * 2,
        compiler_params=pltpu.CompilerParams(vmem_limit_bytes=20 * 2**20),
        cost_estimate=pl.CostEstimate(flops=6 * 10**9, bytes_accessed=8 * 2**20, transcendentals=0),
        name="inner_field",
    )(o, p, mix)


def outer_kernel(e_in, o, halo_low, halo_high, p, plo, phi, mix, e, ace, *scratch):
    g0, g1, g2 = polynomial()
    beta = g2 / g1
    na, nx, ny, nz = p.shape
    nj = o.shape[0]
    steps, halves = ny // STRIP, nz // LANES
    f32, bf = jnp.float32, jnp.bfloat16
    rhos, lefts, bases = scratch[0:2], scratch[2:4], scratch[4:6]
    sides = ((0, halo_low, plo, 1, 0, 0, 1), (1, halo_high, phi, 0, 1, nx - 1, nx - 2))

    def prepare(s, halo, ph, h1, h2, t0, t1):
        rho, left, base = rhos[s], lefts[s], bases[s]
        for i in range(steps):
            for h in range(halves):
                ov = at(halo, (0, h1), i * STRIP, STRIP, h).astype(f32)
                for a in range(na):
                    rho[a, h, PAD + i * STRIP:PAD + (i + 1) * STRIP, :] = at(ph, (a, h1), i * STRIP, STRIP, h).astype(f32) * ov
        for a in range(na):
            wrap(rho, (a,), halves, ny, 1)
        for i in range(steps):
            for h in range(halves):
                r = PAD + i * STRIP
                rows = slice(i * STRIP, (i + 1) * STRIP)
                lanes = slice(h * LANES, (h + 1) * LANES)
                ov = at(halo, (0, h2), i * STRIP, STRIP, h).astype(f32)
                step = None
                for a in range(na):
                    c = sp(rho, (a,), r, STRIP, h)
                    split(left.at[a], rows, nz, h, c)
                    y = sp(rho, (a,), r - 1, STRIP, h) + sp(rho, (a,), r + 1, STRIP, h)
                    base[a, rows, lanes] = (c + beta * (at(ph, (a, h2), i * STRIP, STRIP, h).astype(f32) * ov)) + (2.0 * beta) * y
                    w = at(p, (a, t1), i * STRIP, STRIP, h).astype(f32) * c
                    step = w if step is None else step + w
                e[0, t1, rows, lanes] = at(e_in, (pl.program_id(0), t1), i * STRIP, STRIP, h) + step * (-g1 * beta)

    def finish(s, halo, ph, h1, h2, t0, t1):
        left, base = lefts[s], bases[s]
        mixed = [jnp.dot(left[a], mix[:2 * nz, :], preferred_element_type=f32) for a in range(na)]
        for i in range(steps):
            rows = slice(i * STRIP, (i + 1) * STRIP)
            step = None
            for a in range(na):
                w = p[a, t0, rows, :].astype(f32) * (base[a, rows, :] + (2.0 * beta) * mixed[a][rows])
                step = w if step is None else step + w
            e[0, t0, rows, :] = e_in[pl.program_id(0), t0, rows, :] + step * (-g1)

    prepare(*sides[0])
    prepare(*sides[1])
    finish(*sides[0])
    finish(*sides[1])

    def project(residents):
        sources = [(p, a) for a in range(na)] + [(o, i) for i in range(residents)]

        def one_plane(x, acc):
            acc = list(acc)
            for i in range(steps):
                rows = slice(i * STRIP, (i + 1) * STRIP)
                field = e[0, x, rows, :]
                for s, (ref, n) in enumerate(sources):
                    m = ref[n, x, rows, :].astype(f32) * field
                    m = m[:, :LANES] + m[:, LANES:]
                    acc[s] = acc[s] + jnp.sum(m.reshape(STRIP // 8, 8, LANES), axis=0)
            return tuple(acc)

        acc = lax.fori_loop(0, nx, one_plane, tuple(jnp.zeros((8, LANES), f32) for _ in sources))
        sums = [jnp.sum(a, axis=0, keepdims=True) for a in acc]
        tile = jnp.concatenate(sums + [jnp.zeros((8 - len(sums), LANES), f32)], axis=0)
        share = LANES // nj
        width = LANES // 2
        while width >= share:
            tile = tile + pltpu.roll(tile, width, 1)
            width //= 2
        j = residents - 1
        group = lax.broadcasted_iota(jnp.int32, (8, LANES), 1) // share
        row = lax.broadcasted_iota(jnp.int32, (8, LANES), 0)
        out = jnp.where(group == j, tile, jnp.zeros_like(tile) if j == 0 else ace[...])
        for i in range(j):
            out = jnp.where((group == i) & (row == na + j), tile[na + i:na + i + 1], out)
        ace[...] = out

    for j in range(nj):
        pl.when(pl.program_id(0) == j)(lambda j=j: project(j + 1))


def outer(e, o, halo, p, plo, phi):
    nj, nx, ny, nz = o.shape
    na = p.shape[0]
    g = polynomial()
    f32, bf = jnp.float32, jnp.bfloat16
    mix = mixing(nz, g[2] / g[1])
    each = lambda shape: pl.BlockSpec((1, *shape[1:]), lambda j: (j, *(0,) * (len(shape) - 1)))
    whole = lambda shape: pl.BlockSpec(shape, lambda j: (0,) * len(shape))
    return pl.pallas_call(
        outer_kernel,
        grid=(nj,),
        out_shape=(jax.ShapeDtypeStruct(e.shape, f32), jax.ShapeDtypeStruct((8, LANES), f32)),
        in_specs=[pl.BlockSpec(memory_space=pltpu.VMEM), pl.BlockSpec(memory_space=pltpu.VMEM), *[each(h.shape) for h in halo], pl.BlockSpec(memory_space=pltpu.VMEM), whole(plo.shape), whole(phi.shape), whole(mix.shape)],
        out_specs=(each(e.shape), pl.BlockSpec((8, LANES), lambda j: (0, 0))),
        scratch_shapes=[pltpu.VMEM((na, nz // LANES, ny + 2 * PAD, LANES), f32)] * 2
        + [pltpu.VMEM((na, ny, 2 * nz), bf)] * 2
        + [pltpu.VMEM((na, ny, nz), f32)] * 2,
        compiler_params=pltpu.CompilerParams(vmem_limit_bytes=24 * 2**20),
        cost_estimate=pl.CostEstimate(flops=3 * 10**9, bytes_accessed=14 * 2**20, transcendentals=0),
        name="outer_field",
    )(e, o, *halo, p, plo, phi, mix)


def cut_kernel(row, orbitals, *refs):
    parts = refs[:PANEL * row]
    held, loaded, stored = refs[PANEL * row:]
    x = lax.rem(lax.axis_index("band"), row)
    loads = [pltpu.make_async_copy(orbitals.at[a], held.at[a], loaded.at[a]) for a in range(PANEL)]
    stores = [
        pltpu.make_async_copy(held.at[a, lax.rem(x + k, row)], parts[a * row + k], stored.at[a * row + k])
        for a in range(PANEL)
        for k in range(row)
    ]
    for a in range(PANEL):
        loads[a].start()
    for a in range(PANEL):
        loads[a].wait()
        for k in range(row):
            stores[a * row + k].start()
    for c in stores:
        c.wait()


def cut(orbitals):
    row, ny, nz = orbitals.shape[1:]
    part = jax.ShapeDtypeStruct((ny, nz), orbitals.dtype)
    hbm = pl.BlockSpec(memory_space=pltpu.HBM)
    parts = pl.pallas_call(
        lambda *refs: cut_kernel(row, *refs),
        out_shape=(part,) * (PANEL * row),
        in_specs=[hbm],
        out_specs=(hbm,) * (PANEL * row),
        scratch_shapes=[
            pltpu.VMEM((PANEL, row, ny, nz), orbitals.dtype),
            pltpu.SemaphoreType.DMA((PANEL,)),
            pltpu.SemaphoreType.DMA((PANEL * row,)),
        ],
        name="cut_panel",
    )(orbitals)
    return [parts[a * row:(a + 1) * row] for a in range(PANEL)]


def edges_kernel(orbitals, top, bottom, held, loaded, stored):
    nx = orbitals.shape[1]
    loads = [pltpu.make_async_copy(orbitals.at[:, a:a + 2], held.at[n], loaded.at[n]) for n, a in enumerate((nx - 2, 0))]
    stores = [pltpu.make_async_copy(held.at[n], out, stored.at[n]) for n, out in enumerate((top, bottom))]
    for c in loads:
        c.start()
    for load, store in zip(loads, stores):
        load.wait()
        store.start()
    for c in stores:
        c.wait()


def edges(orbitals):
    nj, _, ny, nz = orbitals.shape
    hbm = pl.BlockSpec(memory_space=pltpu.HBM)
    return pl.pallas_call(
        edges_kernel,
        out_shape=(jax.ShapeDtypeStruct((nj, 2, ny, nz), orbitals.dtype),) * 2,
        in_specs=[hbm],
        out_specs=(hbm, hbm),
        scratch_shapes=[pltpu.VMEM((2, nj, 2, ny, nz), orbitals.dtype), pltpu.SemaphoreType.DMA((2,)), pltpu.SemaphoreType.DMA((2,))],
        name="edge_planes",
    )(orbitals)


def join_kernel(row, *refs):
    parts, (panel, top, bottom, loaded, stored) = refs[:PANEL * row], refs[PANEL * row:]
    x = lax.rem(lax.axis_index("band"), row)
    loads = [
        pltpu.make_async_copy(parts[a * row + k], panel.at[a, lax.rem(x + row - k, row)], loaded.at[a * row + k])
        for a in range(PANEL)
        for k in range(row)
    ]
    stores = [
        pltpu.make_async_copy(panel.at[:, row - 2:], top, stored.at[0]),
        pltpu.make_async_copy(panel.at[:, :2], bottom, stored.at[1]),
    ]
    for c in loads:
        c.start()
    for c in loads:
        c.wait()
    for c in stores:
        c.start()
    for c in stores:
        c.wait()


def join(parts):
    row = len(parts) // PANEL
    ny, nz = parts[0].shape
    dtype = parts[0].dtype
    hbm = pl.BlockSpec(memory_space=pl.ANY)
    edge = pltpu.VMEM((PANEL, 2, ny, nz), dtype)
    return pl.pallas_call(
        lambda *refs: join_kernel(row, *refs),
        out_shape=(pltpu.VMEM((PANEL, row, ny, nz), dtype), edge, edge),
        in_specs=[hbm] * (PANEL * row),
        out_specs=(pl.BlockSpec(memory_space=pltpu.VMEM),) * 3,
        scratch_shapes=[pltpu.SemaphoreType.DMA((PANEL * row,)), pltpu.SemaphoreType.DMA((2,))],
        name="join_panel",
    )(*parts)


def ring(count, shift):
    return [(i, (i + shift) % count) for i in range(count)]


def rows(shift, row):
    count = lax.axis_size("band")
    return [(i, i // row * row + (i + shift) % row) for i in range(count)]


def total(part):
    count = lax.axis_size("dom")
    for group in ((1,), (2,), (4, 8, 12)):
        moved = [lax.ppermute(part, "dom", [(i, i ^ k) for i in range(count)]) for k in group]
        for m in moved:
            part = part + m
    return part


def local(orbitals, owner_band):
    nj, nx, ny, nz = orbitals.shape
    row = nx
    slabs = lax.axis_size("dom")
    me = lax.axis_index("band")
    owner = owner_band[0]
    behind = lax.rem(me + row - lax.rem(owner, row), row)
    same = lax.div(me, row) == lax.div(owner, row)
    up = lambda v: lax.ppermute(v, "dom", ring(lax.axis_size("dom"), 1))
    down = lambda v: lax.ppermute(v, "dom", ring(lax.axis_size("dom"), -1))
    along = lambda v, k: lax.ppermute(v, "band", rows(k, row))
    across = lambda v: lax.ppermute(v, "band", ring(lax.axis_size("band"), row))

    pieces = cut(orbitals)
    o_top, o_bottom = edges(orbitals)
    got = [[pieces[n][0]] + [along(pieces[n][m], m) for m in range(1, row)] for n in range(PANEL)]
    mine = [lax.select_n(behind, *g) for g in got]
    mine[0], o_top, o_bottom = lax.optimization_barrier((mine[0], o_top, o_bottom))
    halo = (up(o_top), down(o_bottom))
    mine = [jnp.where(same, m, across(m)) for m in mine]
    parts = [[m, *[along(m, n) for n in range(1, row)]] for m in mine]
    panel, top, bottom = join(parts[0] + parts[1])
    low, high = up(top), down(bottom)
    exchange, o_wide, p_wide = inner(orbitals, panel)
    exchange, sums = outer(exchange, o_wide, halo, p_wide, low, high)
    cells = float(nx * slabs * ny * nz)
    ace_block = jnp.sum(total(sums)[:PANEL + nj].reshape(PANEL + nj, nj, -1), axis=2) / cells
    return exchange, ace_block[None]


def solution(mesh):
    placed = (P("band", "dom", None, None), P())
    return jax.shard_map(
        local,
        mesh=mesh,
        in_specs=placed,
        out_specs=(P("band", "dom", None, None), P("band", None, None)),
        check_vma=False,
    )
```

```python
import math

import jax
import jax.numpy as jnp
import numpy as np
from jax import lax
from jax.experimental import pallas as pl
from jax.experimental.pallas import tpu as pltpu
from jax.sharding import PartitionSpec as P

PANEL, SWEEPS, SCREEN = 2, 3, 0.1
PAD = 8
STRIP = 32


def polynomial():
    d = 6.0 + SCREEN
    w = [1.0 / (1.0 + 6.0 / d * math.cos(math.pi * (2 * k + 1) / (2 * SWEEPS))) for k in range(SWEEPS)]
    p = [w[0] / d]
    for k in range(1, SWEEPS):
        n = [0.0] * (len(p) + 1)
        for i, c in enumerate(p):
            n[i] += c * (1.0 - w[k])
            n[i + 1] += c * w[k] / d
        n[0] += w[k] / d
        p = n
    return p


def mixing(nz, beta):
    near = np.zeros((nz, nz), np.float32)
    far = np.zeros((nz, nz), np.float32)
    for z in range(nz):
        for s, m in ((1, near), (2, far)):
            m[(z - s) % nz, z] += 1.0
            m[(z + s) % nz, z] += 1.0
    return jnp.asarray(np.concatenate([near, near, beta * far], 0)).astype(jnp.bfloat16)


LANES = 128


def at(ref, idx, start, size, h):
    return ref[(*idx, slice(start, start + size), slice(h * LANES, (h + 1) * LANES))]


def sp(ref, idx, start, size, h):
    return ref[(*idx, h, slice(start, start + size), slice(None))]


def wrap(ref, idx, halves, ny, width):
    for h in range(halves):
        ref[(*idx, h, slice(PAD - width, PAD), slice(None))] = sp(ref, idx, PAD + ny - width, width, h)
        ref[(*idx, h, slice(PAD + ny, PAD + ny + width), slice(None))] = sp(ref, idx, PAD, width, h)


def split(left, rows, nz, h, v):
    hi = v.astype(jnp.bfloat16)
    left[rows, h * LANES:(h + 1) * LANES] = hi
    left[rows, nz + h * LANES:nz + (h + 1) * LANES] = (v - hi.astype(jnp.float32)).astype(jnp.bfloat16)


def inner_kernel(o, p, mix, e, o_wide, p_wide, rho, *scratch):
    j = pl.program_id(0)
    g0, g1, g2 = polynomial()
    beta = g2 / g1
    kappa = g0 / g1 + 6.0 * beta
    na, nx, ny, nz = p.shape
    steps, halves = ny // STRIP, nz // LANES
    f32, bf = jnp.float32, jnp.bfloat16
    sigs, lefts, bases = scratch[0:2], scratch[2:4], scratch[4:6]

    for x in range(nx):
        for i in range(steps):
            for h in range(halves):
                ov = at(o, (0, x), i * STRIP, STRIP, h).astype(f32)
                o_wide[j, x, i * STRIP:(i + 1) * STRIP, h * LANES:(h + 1) * LANES] = ov
                for a in range(na):
                    rho[a, x, h, PAD + i * STRIP:PAD + (i + 1) * STRIP, :] = at(p, (a, x), i * STRIP, STRIP, h).astype(f32) * ov
        for a in range(na):
            wrap(rho, (a, x), halves, ny, 2)

    @pl.when(j == 0)
    def _():
        for a in range(na):
            for x in range(nx):
                for i in range(steps):
                    rows = slice(i * STRIP, (i + 1) * STRIP)
                    p_wide[a, x, rows, :] = p[a, x, rows, :].astype(f32)

    def prepare(x):
        sig, left, base = sigs[x % 2], lefts[x % 2], bases[x % 2]
        near = [n for n in (x - 1, x + 1) if 0 <= n < nx]
        apart = [n for n in (x - 2, x + 2) if 0 <= n < nx]
        if len(near) > 1:
            for a in range(na):
                for h in range(halves):
                    for r in range(0, ny + 2 * PAD, 16):
                        sig[a, h, r:r + 16, :] = sp(rho, (a, near[0]), r, 16, h) + sp(rho, (a, near[1]), r, 16, h)
        for a in range(na):
            s_ref, s_idx = (sig, (a,)) if len(near) > 1 else (rho, (a, near[0]))
            for i in range(steps):
                for h in range(halves):
                    r = PAD + i * STRIP
                    rows = slice(i * STRIP, (i + 1) * STRIP)
                    c = sp(rho, (a, x), r, STRIP, h)
                    q = sp(s_ref, s_idx, r, STRIP, h) + (sp(rho, (a, x), r - 1, STRIP, h) + sp(rho, (a, x), r + 1, STRIP, h))
                    far = sp(rho, (a, x), r - 2, STRIP, h) + sp(rho, (a, x), r + 2, STRIP, h)
                    for n in apart:
                        far = far + sp(rho, (a, n), r, STRIP, h)
                    side = sp(s_ref, s_idx, r - 1, STRIP, h) + sp(s_ref, s_idx, r + 1, STRIP, h)
                    split(left.at[a], rows, nz, h, c + (2.0 * beta) * q)
                    left[a, rows, 2 * nz + h * LANES:2 * nz + (h + 1) * LANES] = c.astype(bf)
                    base[a, rows, h * LANES:(h + 1) * LANES] = (kappa * c + q) + beta * (far + (side + side))

    def finish(x):
        left, base = lefts[x % 2], bases[x % 2]
        mixed = [jnp.dot(left[a], mix[...], preferred_element_type=f32) for a in range(na)]
        for i in range(steps):
            rows = slice(i * STRIP, (i + 1) * STRIP)
            total = None
            for a in range(na):
                w = p[a, x, rows, :].astype(f32) * (base[a, rows, :] + mixed[a][rows])
                total = w if total is None else total + w
            e[pl.program_id(0), x, rows, :] = total * (-g1)

    prepare(0)
    for x in range(1, nx):
        prepare(x)
        finish(x - 1)
    finish(nx - 1)


def inner(o, p):
    nj, nx, ny, nz = o.shape
    na = p.shape[0]
    g = polynomial()
    f32, bf = jnp.float32, jnp.bfloat16
    mix = mixing(nz, g[2] / g[1])
    return pl.pallas_call(
        inner_kernel,
        grid=(nj,),
        out_shape=(pltpu.VMEM((nj, nx, ny, nz), f32), pltpu.VMEM((nj, nx, ny, nz), f32), pltpu.VMEM((na, nx, ny, nz), f32)),
        in_specs=[
            pl.BlockSpec((1, nx, ny, nz), lambda j: (j, 0, 0, 0)),
            pl.BlockSpec(memory_space=pltpu.VMEM),
            pl.BlockSpec(mix.shape, lambda j: (0, 0)),
        ],
        out_specs=(pl.BlockSpec(memory_space=pltpu.VMEM),) * 3,
        scratch_shapes=[pltpu.VMEM((na, nx, nz // LANES, ny + 2 * PAD, LANES), f32)]
        + [pltpu.VMEM((na, nz // LANES, ny + 2 * PAD, LANES), f32)] * 2
        + [pltpu.VMEM((na, ny, 3 * nz), bf)] * 2
        + [pltpu.VMEM((na, ny, nz), f32)] * 2,
        compiler_params=pltpu.CompilerParams(vmem_limit_bytes=20 * 2**20),
        cost_estimate=pl.CostEstimate(flops=6 * 10**9, bytes_accessed=8 * 2**20, transcendentals=0),
        name="inner_field",
    )(o, p, mix)


def outer_kernel(e_in, o, halo_low, halo_high, p, plo, phi, mix, e, ace, *scratch):
    g0, g1, g2 = polynomial()
    beta = g2 / g1
    na, nx, ny, nz = p.shape
    nj = o.shape[0]
    steps, halves = ny // STRIP, nz // LANES
    f32, bf = jnp.float32, jnp.bfloat16
    rhos, lefts, bases = scratch[0:2], scratch[2:4], scratch[4:6]
    sides = ((0, halo_low, plo, 1, 0, 0, 1), (1, halo_high, phi, 0, 1, nx - 1, nx - 2))

    def prepare(s, halo, ph, h1, h2, t0, t1):
        rho, left, base = rhos[s], lefts[s], bases[s]
        for i in range(steps):
            for h in range(halves):
                ov = at(halo, (0, h1), i * STRIP, STRIP, h).astype(f32)
                for a in range(na):
                    rho[a, h, PAD + i * STRIP:PAD + (i + 1) * STRIP, :] = at(ph, (a, h1), i * STRIP, STRIP, h).astype(f32) * ov
        for a in range(na):
            wrap(rho, (a,), halves, ny, 1)
        for i in range(steps):
            for h in range(halves):
                r = PAD + i * STRIP
                rows = slice(i * STRIP, (i + 1) * STRIP)
                lanes = slice(h * LANES, (h + 1) * LANES)
                ov = at(halo, (0, h2), i * STRIP, STRIP, h).astype(f32)
                step = None
                for a in range(na):
                    c = sp(rho, (a,), r, STRIP, h)
                    split(left.at[a], rows, nz, h, c)
                    y = sp(rho, (a,), r - 1, STRIP, h) + sp(rho, (a,), r + 1, STRIP, h)
                    base[a, rows, lanes] = (c + beta * (at(ph, (a, h2), i * STRIP, STRIP, h).astype(f32) * ov)) + (2.0 * beta) * y
                    w = at(p, (a, t1), i * STRIP, STRIP, h).astype(f32) * c
                    step = w if step is None else step + w
                e[0, t1, rows, lanes] = at(e_in, (pl.program_id(0), t1), i * STRIP, STRIP, h) + step * (-g1 * beta)

    def finish(s, halo, ph, h1, h2, t0, t1):
        left, base = lefts[s], bases[s]
        mixed = [jnp.dot(left[a], mix[:2 * nz, :], preferred_element_type=f32) for a in range(na)]
        for i in range(steps):
            rows = slice(i * STRIP, (i + 1) * STRIP)
            step = None
            for a in range(na):
                w = p[a, t0, rows, :].astype(f32) * (base[a, rows, :] + (2.0 * beta) * mixed[a][rows])
                step = w if step is None else step + w
            e[0, t0, rows, :] = e_in[pl.program_id(0), t0, rows, :] + step * (-g1)

    prepare(*sides[0])
    prepare(*sides[1])
    finish(*sides[0])
    finish(*sides[1])

    def project(residents):
        sources = [(p, a) for a in range(na)] + [(o, i) for i in range(residents)]

        def one_plane(x, acc):
            acc = list(acc)
            for i in range(steps):
                rows = slice(i * STRIP, (i + 1) * STRIP)
                field = e[0, x, rows, :]
                for s, (ref, n) in enumerate(sources):
                    m = ref[n, x, rows, :].astype(f32) * field
                    m = m[:, :LANES] + m[:, LANES:]
                    acc[s] = acc[s] + jnp.sum(m.reshape(STRIP // 8, 8, LANES), axis=0)
            return tuple(acc)

        acc = lax.fori_loop(0, nx, one_plane, tuple(jnp.zeros((8, LANES), f32) for _ in sources))
        sums = [jnp.sum(a, axis=0, keepdims=True) for a in acc]
        tile = jnp.concatenate(sums + [jnp.zeros((8 - len(sums), LANES), f32)], axis=0)
        share = LANES // nj
        width = LANES // 2
        while width >= share:
            tile = tile + pltpu.roll(tile, width, 1)
            width //= 2
        j = residents - 1
        group = lax.broadcasted_iota(jnp.int32, (8, LANES), 1) // share
        row = lax.broadcasted_iota(jnp.int32, (8, LANES), 0)
        out = jnp.where(group == j, tile, jnp.zeros_like(tile) if j == 0 else ace[...])
        for i in range(j):
            out = jnp.where((group == i) & (row == na + j), tile[na + i:na + i + 1], out)
        ace[...] = out

    for j in range(nj):
        pl.when(pl.program_id(0) == j)(lambda j=j: project(j + 1))


def outer(e, o, halo, p, plo, phi):
    nj, nx, ny, nz = o.shape
    na = p.shape[0]
    g = polynomial()
    f32, bf = jnp.float32, jnp.bfloat16
    mix = mixing(nz, g[2] / g[1])
    each = lambda shape: pl.BlockSpec((1, *shape[1:]), lambda j: (j, *(0,) * (len(shape) - 1)))
    whole = lambda shape: pl.BlockSpec(shape, lambda j: (0,) * len(shape))
    return pl.pallas_call(
        outer_kernel,
        grid=(nj,),
        out_shape=(jax.ShapeDtypeStruct(e.shape, f32), jax.ShapeDtypeStruct((8, LANES), f32)),
        in_specs=[pl.BlockSpec(memory_space=pltpu.VMEM), pl.BlockSpec(memory_space=pltpu.VMEM), *[each(h.shape) for h in halo], pl.BlockSpec(memory_space=pltpu.VMEM), whole(plo.shape), whole(phi.shape), pl.BlockSpec(memory_space=pltpu.VMEM)],
        out_specs=(each(e.shape), pl.BlockSpec((8, LANES), lambda j: (0, 0))),
        scratch_shapes=[pltpu.VMEM((na, nz // LANES, ny + 2 * PAD, LANES), f32)] * 2
        + [pltpu.VMEM((na, ny, 2 * nz), bf)] * 2
        + [pltpu.VMEM((na, ny, nz), f32)] * 2,
        compiler_params=pltpu.CompilerParams(vmem_limit_bytes=24 * 2**20),
        cost_estimate=pl.CostEstimate(flops=3 * 10**9, bytes_accessed=14 * 2**20, transcendentals=0),
        name="outer_field",
    )(e, o, *halo, p, plo, phi, mix)


def cut_kernel(row, orbitals, *refs):
    parts = refs[:PANEL * row]
    held, loaded, stored = refs[PANEL * row:]
    x = lax.rem(lax.axis_index("band"), row)
    loads = [pltpu.make_async_copy(orbitals.at[a], held.at[a], loaded.at[a]) for a in range(PANEL)]
    stores = [
        pltpu.make_async_copy(held.at[a, lax.rem(x + k, row)], parts[a * row + k], stored.at[a * row + k])
        for a in range(PANEL)
        for k in range(row)
    ]
    for a in range(PANEL):
        loads[a].start()
    for a in range(PANEL):
        loads[a].wait()
        for k in range(row):
            stores[a * row + k].start()
    for c in stores:
        c.wait()


def cut(orbitals):
    row, ny, nz = orbitals.shape[1:]
    part = jax.ShapeDtypeStruct((ny, nz), orbitals.dtype)
    hbm = pl.BlockSpec(memory_space=pltpu.HBM)
    parts = pl.pallas_call(
        lambda *refs: cut_kernel(row, *refs),
        out_shape=(part,) * (PANEL * row),
        in_specs=[hbm],
        out_specs=(hbm,) * (PANEL * row),
        scratch_shapes=[
            pltpu.VMEM((PANEL, row, ny, nz), orbitals.dtype),
            pltpu.SemaphoreType.DMA((PANEL,)),
            pltpu.SemaphoreType.DMA((PANEL * row,)),
        ],
        name="cut_panel",
    )(orbitals)
    return [parts[a * row:(a + 1) * row] for a in range(PANEL)]


def edges_kernel(orbitals, top, bottom, held, loaded, stored):
    nx = orbitals.shape[1]
    loads = [pltpu.make_async_copy(orbitals.at[:, a:a + 2], held.at[n], loaded.at[n]) for n, a in enumerate((nx - 2, 0))]
    stores = [pltpu.make_async_copy(held.at[n], out, stored.at[n]) for n, out in enumerate((top, bottom))]
    for c in loads:
        c.start()
    for load, store in zip(loads, stores):
        load.wait()
        store.start()
    for c in stores:
        c.wait()


def edges(orbitals):
    nj, _, ny, nz = orbitals.shape
    hbm = pl.BlockSpec(memory_space=pltpu.HBM)
    return pl.pallas_call(
        edges_kernel,
        out_shape=(jax.ShapeDtypeStruct((nj, 2, ny, nz), orbitals.dtype),) * 2,
        in_specs=[hbm],
        out_specs=(hbm, hbm),
        scratch_shapes=[pltpu.VMEM((2, nj, 2, ny, nz), orbitals.dtype), pltpu.SemaphoreType.DMA((2,)), pltpu.SemaphoreType.DMA((2,))],
        name="edge_planes",
    )(orbitals)


def join_kernel(row, *refs):
    parts, (panel, top, bottom, loaded, stored) = refs[:row], refs[row:]
    x = lax.rem(lax.axis_index("band"), row)
    loads = [pltpu.make_async_copy(parts[k], panel.at[:, lax.rem(x + row - k, row)], loaded.at[k]) for k in range(row)]
    stores = [
        pltpu.make_async_copy(panel.at[:, row - 2:], top, stored.at[0]),
        pltpu.make_async_copy(panel.at[:, :2], bottom, stored.at[1]),
    ]
    for c in loads:
        c.start()
    for c in loads:
        c.wait()
    for c in stores:
        c.start()
    for c in stores:
        c.wait()


def join(parts):
    row = len(parts)
    _, ny, nz = parts[0].shape
    dtype = parts[0].dtype
    hbm = pl.BlockSpec(memory_space=pl.ANY)
    edge = pltpu.VMEM((PANEL, 2, ny, nz), dtype)
    return pl.pallas_call(
        lambda *refs: join_kernel(row, *refs),
        out_shape=(pltpu.VMEM((PANEL, row, ny, nz), dtype), edge, edge),
        in_specs=[hbm] * row,
        out_specs=(pl.BlockSpec(memory_space=pltpu.VMEM),) * 3,
        scratch_shapes=[pltpu.SemaphoreType.DMA((row,)), pltpu.SemaphoreType.DMA((2,))],
        name="join_panel",
    )(*parts)


def ring(count, shift):
    return [(i, (i + shift) % count) for i in range(count)]


def rows(shift, row):
    count = lax.axis_size("band")
    return [(i, i // row * row + (i + shift) % row) for i in range(count)]


def total(part):
    count = lax.axis_size("dom")
    for group in ((1,), (2,), (4, 8, 12)):
        moved = [lax.ppermute(part, "dom", [(i, i ^ k) for i in range(count)]) for k in group]
        for m in moved:
            part = part + m
    return part


def local(orbitals, owner_band):
    nj, nx, ny, nz = orbitals.shape
    row = nx
    slabs = lax.axis_size("dom")
    me = lax.axis_index("band")
    owner = owner_band[0]
    behind = lax.rem(me + row - lax.rem(owner, row), row)
    same = lax.div(me, row) == lax.div(owner, row)
    up = lambda v: lax.ppermute(v, "dom", ring(lax.axis_size("dom"), 1))
    down = lambda v: lax.ppermute(v, "dom", ring(lax.axis_size("dom"), -1))
    along = lambda v, k: lax.ppermute(v, "band", rows(k, row))
    across = lambda v: lax.ppermute(v, "band", ring(lax.axis_size("band"), row))

    pieces = cut(orbitals)
    o_top, o_bottom = edges(orbitals)
    got = [[pieces[n][0]] + [along(pieces[n][m], m) for m in range(1, row)] for n in range(PANEL)]
    mine = [lax.select_n(behind, *g) for g in got]
    mine[0], o_top, o_bottom = lax.optimization_barrier((mine[0], o_top, o_bottom))
    halo = (up(o_top), down(o_bottom))
    other = [across(m) for m in mine]
    both = jnp.where(same, jnp.stack(mine), jnp.stack(other))
    panel, top, bottom = join([both] + [along(both, n) for n in range(1, row)])
    low, high = up(top), down(bottom)
    exchange, o_wide, p_wide = inner(orbitals, panel)
    exchange, sums = outer(exchange, o_wide, halo, p_wide, low, high)
    cells = float(nx * slabs * ny * nz)
    ace_block = jnp.sum(total(sums)[:PANEL + nj].reshape(PANEL + nj, nj, -1), axis=2) / cells
    return exchange, ace_block[None]


def solution(mesh):
    placed = (P("band", "dom", None, None), P())
    return jax.shard_map(
        local,
        mesh=mesh,
        in_specs=placed,
        out_specs=(P("band", "dom", None, None), P("band", None, None)),
        check_vma=False,
    )
```

```python
import math

import jax
import jax.numpy as jnp
import numpy as np
from jax import lax
from jax.experimental import pallas as pl
from jax.experimental.pallas import tpu as pltpu
from jax.sharding import PartitionSpec as P

PANEL, SWEEPS, SCREEN = 2, 3, 0.1
PAD = 8
STRIP = 32


def polynomial():
    d = 6.0 + SCREEN
    w = [1.0 / (1.0 + 6.0 / d * math.cos(math.pi * (2 * k + 1) / (2 * SWEEPS))) for k in range(SWEEPS)]
    p = [w[0] / d]
    for k in range(1, SWEEPS):
        n = [0.0] * (len(p) + 1)
        for i, c in enumerate(p):
            n[i] += c * (1.0 - w[k])
            n[i + 1] += c * w[k] / d
        n[0] += w[k] / d
        p = n
    return p


def mixing(nz, beta):
    near = np.zeros((nz, nz), np.float32)
    far = np.zeros((nz, nz), np.float32)
    for z in range(nz):
        for s, m in ((1, near), (2, far)):
            m[(z - s) % nz, z] += 1.0
            m[(z + s) % nz, z] += 1.0
    return jnp.asarray(np.concatenate([near, near, beta * far], 0)).astype(jnp.bfloat16)


LANES = 128


def at(ref, idx, start, size, h):
    return ref[(*idx, slice(start, start + size), slice(h * LANES, (h + 1) * LANES))]


def sp(ref, idx, start, size, h):
    return ref[(*idx, h, slice(start, start + size), slice(None))]


def wrap(ref, idx, halves, ny, width):
    for h in range(halves):
        ref[(*idx, h, slice(PAD - width, PAD), slice(None))] = sp(ref, idx, PAD + ny - width, width, h)
        ref[(*idx, h, slice(PAD + ny, PAD + ny + width), slice(None))] = sp(ref, idx, PAD, width, h)


def split(left, rows, nz, h, v):
    hi = v.astype(jnp.bfloat16)
    left[rows, h * LANES:(h + 1) * LANES] = hi
    left[rows, nz + h * LANES:nz + (h + 1) * LANES] = (v - hi.astype(jnp.float32)).astype(jnp.bfloat16)


def inner_kernel(o, p, mix, e, o_wide, p_wide, rho, *scratch):
    j = pl.program_id(0)
    g0, g1, g2 = polynomial()
    beta = g2 / g1
    kappa = g0 / g1 + 6.0 * beta
    na, nx, ny, nz = p.shape
    steps, halves = ny // STRIP, nz // LANES
    f32, bf = jnp.float32, jnp.bfloat16
    sigs, lefts, bases = scratch[0:2], scratch[2:4], scratch[4:6]

    for x in range(nx):
        for i in range(steps):
            for h in range(halves):
                ov = at(o, (0, x), i * STRIP, STRIP, h).astype(f32)
                o_wide[j, x, i * STRIP:(i + 1) * STRIP, h * LANES:(h + 1) * LANES] = ov
                for a in range(na):
                    rho[a, x, h, PAD + i * STRIP:PAD + (i + 1) * STRIP, :] = at(p, (a, x), i * STRIP, STRIP, h).astype(f32) * ov
        for a in range(na):
            wrap(rho, (a, x), halves, ny, 2)

    @pl.when(j == 0)
    def _():
        for a in range(na):
            for x in range(nx):
                for i in range(steps):
                    rows = slice(i * STRIP, (i + 1) * STRIP)
                    p_wide[a, x, rows, :] = p[a, x, rows, :].astype(f32)

    def prepare(x):
        sig, left, base = sigs[x % 2], lefts[x % 2], bases[x % 2]
        near = [n for n in (x - 1, x + 1) if 0 <= n < nx]
        apart = [n for n in (x - 2, x + 2) if 0 <= n < nx]
        if len(near) > 1:
            for a in range(na):
                for h in range(halves):
                    for r in range(0, ny + 2 * PAD, 16):
                        sig[a, h, r:r + 16, :] = sp(rho, (a, near[0]), r, 16, h) + sp(rho, (a, near[1]), r, 16, h)
        for a in range(na):
            s_ref, s_idx = (sig, (a,)) if len(near) > 1 else (rho, (a, near[0]))
            for i in range(steps):
                for h in range(halves):
                    r = PAD + i * STRIP
                    rows = slice(i * STRIP, (i + 1) * STRIP)
                    c = sp(rho, (a, x), r, STRIP, h)
                    q = sp(s_ref, s_idx, r, STRIP, h) + (sp(rho, (a, x), r - 1, STRIP, h) + sp(rho, (a, x), r + 1, STRIP, h))
                    far = sp(rho, (a, x), r - 2, STRIP, h) + sp(rho, (a, x), r + 2, STRIP, h)
                    for n in apart:
                        far = far + sp(rho, (a, n), r, STRIP, h)
                    side = sp(s_ref, s_idx, r - 1, STRIP, h) + sp(s_ref, s_idx, r + 1, STRIP, h)
                    split(left.at[a], rows, nz, h, c + (2.0 * beta) * q)
                    left[a, rows, 2 * nz + h * LANES:2 * nz + (h + 1) * LANES] = c.astype(bf)
                    base[a, rows, h * LANES:(h + 1) * LANES] = (kappa * c + q) + beta * (far + (side + side))

    def finish(x):
        left, base = lefts[x % 2], bases[x % 2]
        mixed = [jnp.dot(left[a], mix[...], preferred_element_type=f32) for a in range(na)]
        for i in range(steps):
            rows = slice(i * STRIP, (i + 1) * STRIP)
            total = None
            for a in range(na):
                w = p[a, x, rows, :].astype(f32) * (base[a, rows, :] + mixed[a][rows])
                total = w if total is None else total + w
            e[pl.program_id(0), x, rows, :] = total * (-g1)

    prepare(0)
    for x in range(1, nx):
        prepare(x)
        finish(x - 1)
    finish(nx - 1)


def inner(o, p):
    nj, nx, ny, nz = o.shape
    na = p.shape[0]
    g = polynomial()
    f32, bf = jnp.float32, jnp.bfloat16
    mix = mixing(nz, g[2] / g[1])
    return pl.pallas_call(
        inner_kernel,
        grid=(nj,),
        out_shape=(pltpu.VMEM((nj, nx, ny, nz), f32), pltpu.VMEM((nj, nx, ny, nz), f32), pltpu.VMEM((na, nx, ny, nz), f32)),
        in_specs=[
            pl.BlockSpec((1, nx, ny, nz), lambda j: (j, 0, 0, 0)),
            pl.BlockSpec(memory_space=pltpu.VMEM),
            pl.BlockSpec(mix.shape, lambda j: (0, 0)),
        ],
        out_specs=(pl.BlockSpec(memory_space=pltpu.VMEM),) * 3,
        scratch_shapes=[pltpu.VMEM((na, nx, nz // LANES, ny + 2 * PAD, LANES), f32)]
        + [pltpu.VMEM((na, nz // LANES, ny + 2 * PAD, LANES), f32)] * 2
        + [pltpu.VMEM((na, ny, 3 * nz), bf)] * 2
        + [pltpu.VMEM((na, ny, nz), f32)] * 2,
        compiler_params=pltpu.CompilerParams(vmem_limit_bytes=20 * 2**20),
        cost_estimate=pl.CostEstimate(flops=6 * 10**9, bytes_accessed=8 * 2**20, transcendentals=0),
        name="inner_field",
    )(o, p, mix)


def outer_kernel(e_in, o, halo_low, halo_high, p, plo, phi, mix, e, ace, *scratch):
    g0, g1, g2 = polynomial()
    beta = g2 / g1
    na, nx, ny, nz = p.shape
    nj = o.shape[0]
    steps, halves = ny // STRIP, nz // LANES
    f32, bf = jnp.float32, jnp.bfloat16
    rhos, lefts, bases = scratch[0:2], scratch[2:4], scratch[4:6]
    sides = ((0, halo_low, plo, 1, 0, 0, 1), (1, halo_high, phi, 0, 1, nx - 1, nx - 2))

    def prepare(s, halo, ph, h1, h2, t0, t1):
        rho, left, base = rhos[s], lefts[s], bases[s]
        for i in range(steps):
            for h in range(halves):
                ov = at(halo, (pl.program_id(0), h1), i * STRIP, STRIP, h).astype(f32)
                for a in range(na):
                    rho[a, h, PAD + i * STRIP:PAD + (i + 1) * STRIP, :] = at(ph, (a, h1), i * STRIP, STRIP, h).astype(f32) * ov
        for a in range(na):
            wrap(rho, (a,), halves, ny, 1)
        for i in range(steps):
            for h in range(halves):
                r = PAD + i * STRIP
                rows = slice(i * STRIP, (i + 1) * STRIP)
                lanes = slice(h * LANES, (h + 1) * LANES)
                ov = at(halo, (pl.program_id(0), h2), i * STRIP, STRIP, h).astype(f32)
                step = None
                for a in range(na):
                    c = sp(rho, (a,), r, STRIP, h)
                    split(left.at[a], rows, nz, h, c)
                    y = sp(rho, (a,), r - 1, STRIP, h) + sp(rho, (a,), r + 1, STRIP, h)
                    base[a, rows, lanes] = (c + beta * (at(ph, (a, h2), i * STRIP, STRIP, h).astype(f32) * ov)) + (2.0 * beta) * y
                    w = at(p, (a, t1), i * STRIP, STRIP, h).astype(f32) * c
                    step = w if step is None else step + w
                e[0, t1, rows, lanes] = at(e_in, (pl.program_id(0), t1), i * STRIP, STRIP, h) + step * (-g1 * beta)

    def finish(s, halo, ph, h1, h2, t0, t1):
        left, base = lefts[s], bases[s]
        mixed = [jnp.dot(left[a], mix[:2 * nz, :], preferred_element_type=f32) for a in range(na)]
        for i in range(steps):
            rows = slice(i * STRIP, (i + 1) * STRIP)
            step = None
            for a in range(na):
                w = p[a, t0, rows, :].astype(f32) * (base[a, rows, :] + (2.0 * beta) * mixed[a][rows])
                step = w if step is None else step + w
            e[0, t0, rows, :] = e_in[pl.program_id(0), t0, rows, :] + step * (-g1)

    prepare(*sides[0])
    prepare(*sides[1])
    finish(*sides[0])
    finish(*sides[1])

    def project(residents):
        sources = [(p, a) for a in range(na)] + [(o, i) for i in range(residents)]

        def one_plane(x, acc):
            acc = list(acc)
            for i in range(steps):
                rows = slice(i * STRIP, (i + 1) * STRIP)
                field = e[0, x, rows, :]
                for s, (ref, n) in enumerate(sources):
                    m = ref[n, x, rows, :].astype(f32) * field
                    m = m[:, :LANES] + m[:, LANES:]
                    acc[s] = acc[s] + jnp.sum(m.reshape(STRIP // 8, 8, LANES), axis=0)
            return tuple(acc)

        acc = lax.fori_loop(0, nx, one_plane, tuple(jnp.zeros((8, LANES), f32) for _ in sources))
        sums = [jnp.sum(a, axis=0, keepdims=True) for a in acc]
        tile = jnp.concatenate(sums + [jnp.zeros((8 - len(sums), LANES), f32)], axis=0)
        share = LANES // nj
        width = LANES // 2
        while width >= share:
            tile = tile + pltpu.roll(tile, width, 1)
            width //= 2
        j = residents - 1
        group = lax.broadcasted_iota(jnp.int32, (8, LANES), 1) // share
        row = lax.broadcasted_iota(jnp.int32, (8, LANES), 0)
        out = jnp.where(group == j, tile, jnp.zeros_like(tile) if j == 0 else ace[...])
        for i in range(j):
            out = jnp.where((group == i) & (row == na + j), tile[na + i:na + i + 1], out)
        ace[...] = out

    for j in range(nj):
        pl.when(pl.program_id(0) == j)(lambda j=j: project(j + 1))


def outer(e, o, halo, p, plo, phi):
    nj, nx, ny, nz = o.shape
    na = p.shape[0]
    g = polynomial()
    f32, bf = jnp.float32, jnp.bfloat16
    mix = mixing(nz, g[2] / g[1])
    each = lambda shape: pl.BlockSpec((1, *shape[1:]), lambda j: (j, *(0,) * (len(shape) - 1)))
    whole = lambda shape: pl.BlockSpec(shape, lambda j: (0,) * len(shape))
    return pl.pallas_call(
        outer_kernel,
        grid=(nj,),
        out_shape=(jax.ShapeDtypeStruct(e.shape, f32), jax.ShapeDtypeStruct((8, LANES), f32)),
        in_specs=[pl.BlockSpec(memory_space=pltpu.VMEM), pl.BlockSpec(memory_space=pltpu.VMEM), *[pl.BlockSpec(memory_space=pltpu.VMEM)] * 2, pl.BlockSpec(memory_space=pltpu.VMEM), whole(plo.shape), whole(phi.shape), pl.BlockSpec(memory_space=pltpu.VMEM)],
        out_specs=(each(e.shape), pl.BlockSpec((8, LANES), lambda j: (0, 0))),
        scratch_shapes=[pltpu.VMEM((na, nz // LANES, ny + 2 * PAD, LANES), f32)] * 2
        + [pltpu.VMEM((na, ny, 2 * nz), bf)] * 2
        + [pltpu.VMEM((na, ny, nz), f32)] * 2,
        compiler_params=pltpu.CompilerParams(vmem_limit_bytes=24 * 2**20),
        cost_estimate=pl.CostEstimate(flops=3 * 10**9, bytes_accessed=14 * 2**20, transcendentals=0),
        name="outer_field",
    )(e, o, *halo, p, plo, phi, mix)


def hold_kernel(low_in, high_in, after, low, high, sems):
    copies = [pltpu.make_async_copy(low_in, low, sems.at[0]), pltpu.make_async_copy(high_in, high, sems.at[1])]
    for c in copies:
        c.start()
    for c in copies:
        c.wait()


def hold(halo, after):
    vmem = pl.BlockSpec(memory_space=pltpu.VMEM)
    return pl.pallas_call(
        hold_kernel,
        out_shape=tuple(pltpu.VMEM(h.shape, h.dtype) for h in halo),
        in_specs=[pl.BlockSpec(memory_space=pl.ANY)] * 2 + [vmem],
        out_specs=(vmem, vmem),
        scratch_shapes=[pltpu.SemaphoreType.DMA((2,))],
        compiler_params=pltpu.CompilerParams(vmem_limit_bytes=2**20),
        name="hold_halo",
    )(*halo, after)


def cut_kernel(row, orbitals, *refs):
    parts = refs[:PANEL * row]
    held, loaded, stored = refs[PANEL * row:]
    x = lax.rem(lax.axis_index("band"), row)
    loads = [pltpu.make_async_copy(orbitals.at[a], held.at[a], loaded.at[a]) for a in range(PANEL)]
    stores = [
        pltpu.make_async_copy(held.at[a, lax.rem(x + k, row)], parts[a * row + k], stored.at[a * row + k])
        for a in range(PANEL)
        for k in range(row)
    ]
    for a in range(PANEL):
        loads[a].start()
    for a in range(PANEL):
        loads[a].wait()
        for k in range(row):
            stores[a * row + k].start()
    for c in stores:
        c.wait()


def cut(orbitals):
    row, ny, nz = orbitals.shape[1:]
    part = jax.ShapeDtypeStruct((ny, nz), orbitals.dtype)
    hbm = pl.BlockSpec(memory_space=pltpu.HBM)
    parts = pl.pallas_call(
        lambda *refs: cut_kernel(row, *refs),
        out_shape=(part,) * (PANEL * row),
        in_specs=[hbm],
        out_specs=(hbm,) * (PANEL * row),
        scratch_shapes=[
            pltpu.VMEM((PANEL, row, ny, nz), orbitals.dtype),
            pltpu.SemaphoreType.DMA((PANEL,)),
            pltpu.SemaphoreType.DMA((PANEL * row,)),
        ],
        name="cut_panel",
    )(orbitals)
    return [parts[a * row:(a + 1) * row] for a in range(PANEL)]


def edges_kernel(orbitals, top, bottom, held, loaded, stored):
    nx = orbitals.shape[1]
    loads = [pltpu.make_async_copy(orbitals.at[:, a:a + 2], held.at[n], loaded.at[n]) for n, a in enumerate((nx - 2, 0))]
    stores = [pltpu.make_async_copy(held.at[n], out, stored.at[n]) for n, out in enumerate((top, bottom))]
    for c in loads:
        c.start()
    for load, store in zip(loads, stores):
        load.wait()
        store.start()
    for c in stores:
        c.wait()


def edges(orbitals):
    nj, _, ny, nz = orbitals.shape
    hbm = pl.BlockSpec(memory_space=pltpu.HBM)
    return pl.pallas_call(
        edges_kernel,
        out_shape=(jax.ShapeDtypeStruct((nj, 2, ny, nz), orbitals.dtype),) * 2,
        in_specs=[hbm],
        out_specs=(hbm, hbm),
        scratch_shapes=[pltpu.VMEM((2, nj, 2, ny, nz), orbitals.dtype), pltpu.SemaphoreType.DMA((2,)), pltpu.SemaphoreType.DMA((2,))],
        name="edge_planes",
    )(orbitals)


def join_kernel(row, *refs):
    parts, (panel, top, bottom, loaded, stored) = refs[:row], refs[row:]
    x = lax.rem(lax.axis_index("band"), row)
    loads = [pltpu.make_async_copy(parts[k], panel.at[:, lax.rem(x + row - k, row)], loaded.at[k]) for k in range(row)]
    stores = [
        pltpu.make_async_copy(panel.at[:, row - 2:], top, stored.at[0]),
        pltpu.make_async_copy(panel.at[:, :2], bottom, stored.at[1]),
    ]
    for c in loads:
        c.start()
    for c in loads:
        c.wait()
    for c in stores:
        c.start()
    for c in stores:
        c.wait()


def join(parts):
    row = len(parts)
    _, ny, nz = parts[0].shape
    dtype = parts[0].dtype
    hbm = pl.BlockSpec(memory_space=pl.ANY)
    edge = pltpu.VMEM((PANEL, 2, ny, nz), dtype)
    return pl.pallas_call(
        lambda *refs: join_kernel(row, *refs),
        out_shape=(pltpu.VMEM((PANEL, row, ny, nz), dtype), edge, edge),
        in_specs=[hbm] * row,
        out_specs=(pl.BlockSpec(memory_space=pltpu.VMEM),) * 3,
        scratch_shapes=[pltpu.SemaphoreType.DMA((row,)), pltpu.SemaphoreType.DMA((2,))],
        name="join_panel",
    )(*parts)


def ring(count, shift):
    return [(i, (i + shift) % count) for i in range(count)]


def rows(shift, row):
    count = lax.axis_size("band")
    return [(i, i // row * row + (i + shift) % row) for i in range(count)]


def total(part):
    count = lax.axis_size("dom")
    for group in ((1,), (2,), (4, 8, 12)):
        moved = [lax.ppermute(part, "dom", [(i, i ^ k) for i in range(count)]) for k in group]
        for m in moved:
            part = part + m
    return part


def local(orbitals, owner_band):
    nj, nx, ny, nz = orbitals.shape
    row = nx
    slabs = lax.axis_size("dom")
    me = lax.axis_index("band")
    owner = owner_band[0]
    behind = lax.rem(me + row - lax.rem(owner, row), row)
    same = lax.div(me, row) == lax.div(owner, row)
    up = lambda v: lax.ppermute(v, "dom", ring(lax.axis_size("dom"), 1))
    down = lambda v: lax.ppermute(v, "dom", ring(lax.axis_size("dom"), -1))
    along = lambda v, k: lax.ppermute(v, "band", rows(k, row))
    across = lambda v: lax.ppermute(v, "band", ring(lax.axis_size("band"), row))

    pieces = cut(orbitals)
    o_top, o_bottom = edges(orbitals)
    got = [[pieces[n][0]] + [along(pieces[n][m], m) for m in range(1, row)] for n in range(PANEL)]
    mine = [lax.select_n(behind, *g) for g in got]
    mine[0], o_top, o_bottom = lax.optimization_barrier((mine[0], o_top, o_bottom))
    halo = (up(o_top), down(o_bottom))
    other = [across(m) for m in mine]
    both = jnp.where(same, jnp.stack(mine), jnp.stack(other))
    panel, top, bottom = join([both] + [along(both, n) for n in range(1, row)])
    low, high = up(top), down(bottom)
    exchange, o_wide, p_wide = inner(orbitals, panel)
    halo = hold(halo, p_wide)
    exchange, sums = outer(exchange, o_wide, halo, p_wide, low, high)
    cells = float(nx * slabs * ny * nz)
    ace_block = jnp.sum(total(sums)[:PANEL + nj].reshape(PANEL + nj, nj, -1), axis=2) / cells
    return exchange, ace_block[None]


def solution(mesh):
    placed = (P("band", "dom", None, None), P())
    return jax.shard_map(
        local,
        mesh=mesh,
        in_specs=placed,
        out_specs=(P("band", "dom", None, None), P("band", None, None)),
        check_vma=False,
    )
```

```python
import math

import jax
import jax.numpy as jnp
import numpy as np
from jax import lax
from jax.experimental import pallas as pl
from jax.experimental.pallas import tpu as pltpu
from jax.sharding import PartitionSpec as P

PANEL, SWEEPS, SCREEN = 2, 3, 0.1
PAD = 8
STRIP = 32


def polynomial():
    d = 6.0 + SCREEN
    w = [1.0 / (1.0 + 6.0 / d * math.cos(math.pi * (2 * k + 1) / (2 * SWEEPS))) for k in range(SWEEPS)]
    p = [w[0] / d]
    for k in range(1, SWEEPS):
        n = [0.0] * (len(p) + 1)
        for i, c in enumerate(p):
            n[i] += c * (1.0 - w[k])
            n[i + 1] += c * w[k] / d
        n[0] += w[k] / d
        p = n
    return p


def mixing(nz, beta):
    near = np.zeros((nz, nz), np.float32)
    far = np.zeros((nz, nz), np.float32)
    for z in range(nz):
        for s, m in ((1, near), (2, far)):
            m[(z - s) % nz, z] += 1.0
            m[(z + s) % nz, z] += 1.0
    return jnp.asarray(np.concatenate([near, near, beta * far], 0)).astype(jnp.bfloat16)


LANES = 128


def at(ref, idx, start, size, h):
    return ref[(*idx, slice(start, start + size), slice(h * LANES, (h + 1) * LANES))]


def sp(ref, idx, start, size, h):
    return ref[(*idx, h, slice(start, start + size), slice(None))]


def wrap(ref, idx, halves, ny, width):
    for h in range(halves):
        ref[(*idx, h, slice(PAD - width, PAD), slice(None))] = sp(ref, idx, PAD + ny - width, width, h)
        ref[(*idx, h, slice(PAD + ny, PAD + ny + width), slice(None))] = sp(ref, idx, PAD, width, h)


def split(left, rows, nz, h, v):
    hi = v.astype(jnp.bfloat16)
    left[rows, h * LANES:(h + 1) * LANES] = hi
    left[rows, nz + h * LANES:nz + (h + 1) * LANES] = (v - hi.astype(jnp.float32)).astype(jnp.bfloat16)


def inner_kernel(o, p, mix, e, o_wide, p_wide, rho, *scratch):
    j = pl.program_id(0)
    g0, g1, g2 = polynomial()
    beta = g2 / g1
    kappa = g0 / g1 + 6.0 * beta
    na, nx, ny, nz = p.shape
    steps, halves = ny // STRIP, nz // LANES
    f32, bf = jnp.float32, jnp.bfloat16
    sigs, lefts, bases = scratch[0:2], scratch[2:4], scratch[4:6]

    for x in range(nx):
        for i in range(steps):
            for h in range(halves):
                ov = at(o, (0, x), i * STRIP, STRIP, h).astype(f32)
                o_wide[j, x, i * STRIP:(i + 1) * STRIP, h * LANES:(h + 1) * LANES] = ov
                for a in range(na):
                    rho[a, x, h, PAD + i * STRIP:PAD + (i + 1) * STRIP, :] = at(p, (a, x), i * STRIP, STRIP, h).astype(f32) * ov
        for a in range(na):
            wrap(rho, (a, x), halves, ny, 2)

    @pl.when(j == 0)
    def _():
        for a in range(na):
            for x in range(nx):
                for i in range(steps):
                    rows = slice(i * STRIP, (i + 1) * STRIP)
                    p_wide[a, x, rows, :] = p[a, x, rows, :].astype(f32)

    def prepare(x):
        sig, left, base = sigs[x % 2], lefts[x % 2], bases[x % 2]
        near = [n for n in (x - 1, x + 1) if 0 <= n < nx]
        apart = [n for n in (x - 2, x + 2) if 0 <= n < nx]
        if len(near) > 1:
            for a in range(na):
                for h in range(halves):
                    for r in range(0, ny + 2 * PAD, 16):
                        sig[a, h, r:r + 16, :] = sp(rho, (a, near[0]), r, 16, h) + sp(rho, (a, near[1]), r, 16, h)
        for a in range(na):
            s_ref, s_idx = (sig, (a,)) if len(near) > 1 else (rho, (a, near[0]))
            for i in range(steps):
                for h in range(halves):
                    r = PAD + i * STRIP
                    rows = slice(i * STRIP, (i + 1) * STRIP)
                    c = sp(rho, (a, x), r, STRIP, h)
                    q = sp(s_ref, s_idx, r, STRIP, h) + (sp(rho, (a, x), r - 1, STRIP, h) + sp(rho, (a, x), r + 1, STRIP, h))
                    far = sp(rho, (a, x), r - 2, STRIP, h) + sp(rho, (a, x), r + 2, STRIP, h)
                    for n in apart:
                        far = far + sp(rho, (a, n), r, STRIP, h)
                    side = sp(s_ref, s_idx, r - 1, STRIP, h) + sp(s_ref, s_idx, r + 1, STRIP, h)
                    split(left.at[a], rows, nz, h, c + (2.0 * beta) * q)
                    left[a, rows, 2 * nz + h * LANES:2 * nz + (h + 1) * LANES] = c.astype(bf)
                    base[a, rows, h * LANES:(h + 1) * LANES] = (kappa * c + q) + beta * (far + (side + side))

    def finish(x):
        left, base = lefts[x % 2], bases[x % 2]
        mixed = [jnp.dot(left[a], mix[...], preferred_element_type=f32) for a in range(na)]
        for i in range(steps):
            rows = slice(i * STRIP, (i + 1) * STRIP)
            total = None
            for a in range(na):
                w = p[a, x, rows, :].astype(f32) * (base[a, rows, :] + mixed[a][rows])
                total = w if total is None else total + w
            e[pl.program_id(0), x, rows, :] = total * (-g1)

    prepare(0)
    for x in range(1, nx):
        prepare(x)
        finish(x - 1)
    finish(nx - 1)


def inner(o, p):
    nj, nx, ny, nz = o.shape
    na = p.shape[0]
    g = polynomial()
    f32, bf = jnp.float32, jnp.bfloat16
    mix = mixing(nz, g[2] / g[1])
    return pl.pallas_call(
        inner_kernel,
        grid=(nj,),
        out_shape=(pltpu.VMEM((nj, nx, ny, nz), f32), pltpu.VMEM((nj, nx, ny, nz), f32), pltpu.VMEM((na, nx, ny, nz), f32)),
        in_specs=[
            pl.BlockSpec((1, nx, ny, nz), lambda j: (j, 0, 0, 0)),
            pl.BlockSpec(memory_space=pltpu.VMEM),
            pl.BlockSpec(mix.shape, lambda j: (0, 0)),
        ],
        out_specs=(pl.BlockSpec(memory_space=pltpu.VMEM),) * 3,
        scratch_shapes=[pltpu.VMEM((na, nx, nz // LANES, ny + 2 * PAD, LANES), f32)]
        + [pltpu.VMEM((na, nz // LANES, ny + 2 * PAD, LANES), f32)] * 2
        + [pltpu.VMEM((na, ny, 3 * nz), bf)] * 2
        + [pltpu.VMEM((na, ny, nz), f32)] * 2,
        compiler_params=pltpu.CompilerParams(vmem_limit_bytes=20 * 2**20),
        cost_estimate=pl.CostEstimate(flops=6 * 10**9, bytes_accessed=8 * 2**20, transcendentals=0),
        name="inner_field",
    )(o, p, mix)


def outer_kernel(e_in, o, halo_low, halo_high, p, plo, phi, mix, e, ace, *scratch):
    g0, g1, g2 = polynomial()
    beta = g2 / g1
    na, nx, ny, nz = p.shape
    nj = o.shape[0]
    steps, halves = ny // STRIP, nz // LANES
    f32, bf = jnp.float32, jnp.bfloat16
    rhos, lefts, bases = scratch[0:2], scratch[2:4], scratch[4:6]
    sides = ((0, halo_low, plo, 1, 0, 0, 1), (1, halo_high, phi, 0, 1, nx - 1, nx - 2))

    def prepare(s, halo, ph, h1, h2, t0, t1):
        rho, left, base = rhos[s], lefts[s], bases[s]
        for i in range(steps):
            for h in range(halves):
                ov = at(halo, (0, h1), i * STRIP, STRIP, h).astype(f32)
                for a in range(na):
                    rho[a, h, PAD + i * STRIP:PAD + (i + 1) * STRIP, :] = at(ph, (a, h1), i * STRIP, STRIP, h).astype(f32) * ov
        for a in range(na):
            wrap(rho, (a,), halves, ny, 1)
        for i in range(steps):
            for h in range(halves):
                r = PAD + i * STRIP
                rows = slice(i * STRIP, (i + 1) * STRIP)
                lanes = slice(h * LANES, (h + 1) * LANES)
                ov = at(halo, (0, h2), i * STRIP, STRIP, h).astype(f32)
                step = None
                for a in range(na):
                    c = sp(rho, (a,), r, STRIP, h)
                    split(left.at[a], rows, nz, h, c)
                    y = sp(rho, (a,), r - 1, STRIP, h) + sp(rho, (a,), r + 1, STRIP, h)
                    base[a, rows, lanes] = (c + beta * (at(ph, (a, h2), i * STRIP, STRIP, h).astype(f32) * ov)) + (2.0 * beta) * y
                    w = at(p, (a, t1), i * STRIP, STRIP, h).astype(f32) * c
                    step = w if step is None else step + w
                e[0, t1, rows, lanes] = at(e_in, (pl.program_id(0), t1), i * STRIP, STRIP, h) + step * (-g1 * beta)

    def finish(s, halo, ph, h1, h2, t0, t1):
        left, base = lefts[s], bases[s]
        mixed = [jnp.dot(left[a], mix[:2 * nz, :], preferred_element_type=f32) for a in range(na)]
        for i in range(steps):
            rows = slice(i * STRIP, (i + 1) * STRIP)
            step = None
            for a in range(na):
                w = p[a, t0, rows, :].astype(f32) * (base[a, rows, :] + (2.0 * beta) * mixed[a][rows])
                step = w if step is None else step + w
            e[0, t0, rows, :] = e_in[pl.program_id(0), t0, rows, :] + step * (-g1)

    prepare(*sides[0])
    prepare(*sides[1])
    finish(*sides[0])
    finish(*sides[1])

    def project(residents):
        sources = [(p, a) for a in range(na)] + [(o, i) for i in range(residents)]

        def one_plane(x, acc):
            acc = list(acc)
            for i in range(steps):
                rows = slice(i * STRIP, (i + 1) * STRIP)
                field = e[0, x, rows, :]
                for s, (ref, n) in enumerate(sources):
                    m = ref[n, x, rows, :].astype(f32) * field
                    m = m[:, :LANES] + m[:, LANES:]
                    acc[s] = acc[s] + jnp.sum(m.reshape(STRIP // 8, 8, LANES), axis=0)
            return tuple(acc)

        acc = lax.fori_loop(0, nx, one_plane, tuple(jnp.zeros((8, LANES), f32) for _ in sources))
        sums = [jnp.sum(a, axis=0, keepdims=True) for a in acc]
        tile = jnp.concatenate(sums + [jnp.zeros((8 - len(sums), LANES), f32)], axis=0)
        share = LANES // nj
        width = LANES // 2
        while width >= share:
            tile = tile + pltpu.roll(tile, width, 1)
            width //= 2
        j = residents - 1
        group = lax.broadcasted_iota(jnp.int32, (8, LANES), 1) // share
        row = lax.broadcasted_iota(jnp.int32, (8, LANES), 0)
        out = jnp.where(group == j, tile, jnp.zeros_like(tile) if j == 0 else ace[...])
        for i in range(j):
            out = jnp.where((group == i) & (row == na + j), tile[na + i:na + i + 1], out)
        ace[...] = out

    for j in range(nj):
        pl.when(pl.program_id(0) == j)(lambda j=j: project(j + 1))


def outer(e, o, halo, p, plo, phi):
    nj, nx, ny, nz = o.shape
    na = p.shape[0]
    g = polynomial()
    f32, bf = jnp.float32, jnp.bfloat16
    mix = mixing(nz, g[2] / g[1])
    each = lambda shape: pl.BlockSpec((1, *shape[1:]), lambda j: (j, *(0,) * (len(shape) - 1)))
    whole = lambda shape: pl.BlockSpec(shape, lambda j: (0,) * len(shape))
    return pl.pallas_call(
        outer_kernel,
        grid=(nj,),
        out_shape=(jax.ShapeDtypeStruct(e.shape, f32), jax.ShapeDtypeStruct((8, LANES), f32)),
        in_specs=[pl.BlockSpec(memory_space=pltpu.VMEM), pl.BlockSpec(memory_space=pltpu.VMEM), *[each(h.shape) for h in halo], pl.BlockSpec(memory_space=pltpu.VMEM), whole(plo.shape), whole(phi.shape), pl.BlockSpec(memory_space=pltpu.VMEM)],
        out_specs=(each(e.shape), pl.BlockSpec((8, LANES), lambda j: (0, 0))),
        scratch_shapes=[pltpu.VMEM((na, nz // LANES, ny + 2 * PAD, LANES), f32)] * 2
        + [pltpu.VMEM((na, ny, 2 * nz), bf)] * 2
        + [pltpu.VMEM((na, ny, nz), f32)] * 2,
        compiler_params=pltpu.CompilerParams(vmem_limit_bytes=24 * 2**20),
        cost_estimate=pl.CostEstimate(flops=3 * 10**9, bytes_accessed=14 * 2**20, transcendentals=0),
        name="outer_field",
    )(e, o, *halo, p, plo, phi, mix)


def cut_kernel(row, orbitals, *refs):
    parts = refs[:PANEL * row]
    held, loaded, stored = refs[PANEL * row:]
    x = lax.rem(lax.axis_index("band"), row)
    loads = [pltpu.make_async_copy(orbitals.at[a], held.at[a], loaded.at[a]) for a in range(PANEL)]
    stores = [
        pltpu.make_async_copy(held.at[a, lax.rem(x + k, row)], parts[a * row + k], stored.at[a * row + k])
        for a in range(PANEL)
        for k in range(row)
    ]
    for a in range(PANEL):
        loads[a].start()
    for a in range(PANEL):
        loads[a].wait()
        for k in range(row):
            stores[a * row + k].start()
    for c in stores:
        c.wait()


def cut(orbitals):
    row, ny, nz = orbitals.shape[1:]
    part = jax.ShapeDtypeStruct((ny, nz), orbitals.dtype)
    hbm = pl.BlockSpec(memory_space=pltpu.HBM)
    parts = pl.pallas_call(
        lambda *refs: cut_kernel(row, *refs),
        out_shape=(part,) * (PANEL * row),
        in_specs=[hbm],
        out_specs=(hbm,) * (PANEL * row),
        scratch_shapes=[
            pltpu.VMEM((PANEL, row, ny, nz), orbitals.dtype),
            pltpu.SemaphoreType.DMA((PANEL,)),
            pltpu.SemaphoreType.DMA((PANEL * row,)),
        ],
        name="cut_panel",
    )(orbitals)
    return [parts[a * row:(a + 1) * row] for a in range(PANEL)]


def edges_kernel(orbitals, top, bottom, loaded):
    nx = orbitals.shape[1]
    loads = [pltpu.make_async_copy(orbitals.at[:, x:x + 2], out, loaded.at[n]) for n, (x, out) in enumerate(((nx - 2, top), (0, bottom)))]
    for c in loads:
        c.start()
    for c in loads:
        c.wait()


def edges(orbitals):
    nj, _, ny, nz = orbitals.shape
    vmem = pl.BlockSpec(memory_space=pltpu.VMEM)
    return pl.pallas_call(
        edges_kernel,
        out_shape=(pltpu.VMEM((nj, 2, ny, nz), orbitals.dtype),) * 2,
        in_specs=[pl.BlockSpec(memory_space=pltpu.HBM)],
        out_specs=(vmem, vmem),
        scratch_shapes=[pltpu.SemaphoreType.DMA((2,))],
        name="edge_planes",
    )(orbitals)


def join_kernel(row, *refs):
    parts, (panel, top, bottom, loaded, stored) = refs[:row], refs[row:]
    x = lax.rem(lax.axis_index("band"), row)
    loads = [pltpu.make_async_copy(parts[k], panel.at[:, lax.rem(x + row - k, row)], loaded.at[k]) for k in range(row)]
    stores = [
        pltpu.make_async_copy(panel.at[:, row - 2:], top, stored.at[0]),
        pltpu.make_async_copy(panel.at[:, :2], bottom, stored.at[1]),
    ]
    for c in loads:
        c.start()
    for c in loads:
        c.wait()
    for c in stores:
        c.start()
    for c in stores:
        c.wait()


def join(parts):
    row = len(parts)
    _, ny, nz = parts[0].shape
    dtype = parts[0].dtype
    hbm = pl.BlockSpec(memory_space=pl.ANY)
    edge = pltpu.VMEM((PANEL, 2, ny, nz), dtype)
    return pl.pallas_call(
        lambda *refs: join_kernel(row, *refs),
        out_shape=(pltpu.VMEM((PANEL, row, ny, nz), dtype), edge, edge),
        in_specs=[hbm] * row,
        out_specs=(pl.BlockSpec(memory_space=pltpu.VMEM),) * 3,
        scratch_shapes=[pltpu.SemaphoreType.DMA((row,)), pltpu.SemaphoreType.DMA((2,))],
        name="join_panel",
    )(*parts)


def ring(count, shift):
    return [(i, (i + shift) % count) for i in range(count)]


def rows(shift, row):
    count = lax.axis_size("band")
    return [(i, i // row * row + (i + shift) % row) for i in range(count)]


def total(part):
    count = lax.axis_size("dom")
    for group in ((1,), (2,), (4, 8, 12)):
        moved = [lax.ppermute(part, "dom", [(i, i ^ k) for i in range(count)]) for k in group]
        for m in moved:
            part = part + m
    return part


def local(orbitals, owner_band):
    nj, nx, ny, nz = orbitals.shape
    row = nx
    slabs = lax.axis_size("dom")
    me = lax.axis_index("band")
    owner = owner_band[0]
    behind = lax.rem(me + row - lax.rem(owner, row), row)
    same = lax.div(me, row) == lax.div(owner, row)
    up = lambda v: lax.ppermute(v, "dom", ring(lax.axis_size("dom"), 1))
    down = lambda v: lax.ppermute(v, "dom", ring(lax.axis_size("dom"), -1))
    along = lambda v, k: lax.ppermute(v, "band", rows(k, row))
    across = lambda v: lax.ppermute(v, "band", ring(lax.axis_size("band"), row))

    pieces = cut(orbitals)
    o_top, o_bottom = edges(orbitals)
    got = [[pieces[n][0]] + [along(pieces[n][m], m) for m in range(1, row)] for n in range(PANEL)]
    mine = [lax.select_n(behind, *g) for g in got]
    mine[0], o_top, o_bottom = lax.optimization_barrier((mine[0], o_top, o_bottom))
    halo = (up(o_top), down(o_bottom))
    other = [across(m) for m in mine]
    both = jnp.where(same, jnp.stack(mine), jnp.stack(other))
    panel, top, bottom = join([both] + [along(both, n) for n in range(1, row)])
    low, high = up(top), down(bottom)
    exchange, o_wide, p_wide = inner(orbitals, panel)
    exchange, sums = outer(exchange, o_wide, halo, p_wide, low, high)
    cells = float(nx * slabs * ny * nz)
    ace_block = jnp.sum(total(sums)[:PANEL + nj].reshape(PANEL + nj, nj, -1), axis=2) / cells
    return exchange, ace_block[None]


def solution(mesh):
    placed = (P("band", "dom", None, None), P())
    return jax.shard_map(
        local,
        mesh=mesh,
        in_specs=placed,
        out_specs=(P("band", "dom", None, None), P("band", None, None)),
        check_vma=False,
    )
```
